256 devices in a mesh: seq: 32 (over z, x), head: 8 (over y, core).
Axes of the slice: x: 4, y: 4, z: 8, core: 2. Of those that a mesh axis runs over, the one named last changes fastest.
Arguments:
- queries: bfloat16 [2, 16384, 4096], P(None, 'seq', 'head'), may hold values from -50 to 50
- keys: bfloat16 [2, 16384, 1024], P(None, 'seq', 'head'), may hold values from -6 to 6
- values: bfloat16 [2, 16384, 1024], P(None, 'seq', 'head'), may hold values from -6 to 6
- selected: int32 [2, 32, 32, 3], P(None, 'seq', 'head'), may hold values from 0 to 63, as said below
- length: int32 [1], replicated, may hold values from 16384 to 32768
- out_weight: bfloat16 [4096, 4096], P('head'), may hold values from -0.09375 to 0.09375
Outputs:
- attended: bfloat16 [2, 16384, 4096], P(None, 'seq', 'head')
- projected: bfloat16 [2, 16384, 4096], P(None, ('seq', 'head'))
The draws below stay inside these ranges and needn't reach their ends.
Inputs may be any that keep to these rules, and one draw needn't show every extreme that they name: `selected`: entry [r, s, h, j] belongs to query block b = r * 32 + s. It is an earlier block, or b itself, which selects no block. The earlier blocks among a head's 3 entries are distinct. For each s and each aligned group of 4 heads, over all r, those heads and j, at most 1 entries name earlier blocks of one same residue modulo 32.
All inputs are finite; a program needn't handle non-finite values.
Results may differ from the reference program's by a relative error of at most 0.02.
Values may be sent and summed in bfloat16 or wider, within the bound.
A program may use at most 128 MiB of HBM per device.

```python
import jax
import jax.numpy as jnp
from jax import lax

HEADS = 32
KV_HEADS = 8
HEAD = 128
MODEL = 4096
BLOCK = 512
TOPK = 3
ROUNDS = 2
TOKENS = 32768
N_SEQ = 32
N_HEAD = 8


def draw_queries(key, part):
    key = jax.random.fold_in(key, 101)
    first_key = jax.random.fold_in(key, 0)
    array_shape = (ROUNDS, N_SEQ * BLOCK, HEADS * HEAD)
    result_draw = jnp.clip(jax.random.normal(first_key, array_shape, jnp.float32) * 2.5, -15.0, 15.0)
    return result_draw.astype(jnp.bfloat16)


def draw_keys(key, part):
    key = jax.random.fold_in(key, 202)
    first_key = jax.random.fold_in(key, 0)
    array_shape = (ROUNDS, N_SEQ * BLOCK, KV_HEADS * HEAD)
    result_draw = jnp.clip(jax.random.normal(first_key, array_shape, jnp.float32), -6.0, 6.0)
    return result_draw.astype(jnp.bfloat16)


def draw_selected(key, part):
    key = jax.random.fold_in(key, 303)
    per_group = HEADS // N_HEAD
    asks = ROUNDS * per_group * TOPK
    last_spot = (asks - 1) % N_SEQ
    hot_key, order_key, round_key = jax.random.split(key, 3)
    hottest = jax.random.randint(hot_key, (N_HEAD,), 0, N_SEQ)

    def one_source(source, member):
        mixed_key = jax.random.fold_in(jax.random.fold_in(order_key, source), member)
        shuffled = jax.random.permutation(mixed_key, N_SEQ).astype(jnp.int32)
        wanted = hottest[member]
        where_hot = jnp.argmax(shuffled == wanted)
        displaced = shuffled[last_spot]
        shuffled = shuffled.at[where_hot].set(displaced).at[last_spot].set(wanted)
        ask_order = jnp.arange(asks, dtype=jnp.int32)
        target = shuffled[ask_order % N_SEQ]
        round_now = ask_order // (per_group * TOPK)
        round_limit = jnp.where(target < source, round_now, round_now - 1)
        pick_key = jax.random.fold_in(jax.random.fold_in(round_key, source), member)
        picked = jax.random.randint(pick_key, (asks,), 0, jnp.maximum(round_limit, 0) + 1)
        entries = jnp.where(round_limit >= 0, picked * N_SEQ + target, round_now * N_SEQ + source)
        return entries.reshape(ROUNDS, per_group, TOPK)

    def one_row(source):
        return jax.vmap(lambda member: one_source(source, member))(jnp.arange(N_HEAD, dtype=jnp.int32))
    choice_table = jax.vmap(one_row)(jnp.arange(N_SEQ, dtype=jnp.int32))
    return choice_table.transpose(2, 0, 1, 3, 4).reshape(ROUNDS, N_SEQ, HEADS, TOPK).astype(jnp.int32)


def levels(own_key, dims, pieces, low, largest):
    loudness = 1.0
    for axis_at, shards_of in pieces:
        heights = jax.random.uniform(jax.random.fold_in(jax.random.fold_in(own_key, 6), axis_at), (shards_of,), jnp.float32, low / len(pieces), largest / len(pieces))
        loudness = loudness * jnp.repeat(jnp.exp(heights), dims[axis_at] // shards_of).reshape((-1,) + (1,) * (len(dims) - 1 - axis_at))
    return loudness


def noise(own_key, extent, spread, most, cuts=(), kind=jnp.bfloat16):
    values = jax.random.normal(own_key, extent, jnp.float32) * spread
    if len(cuts) > 0:
        values = levels(own_key, extent, cuts, -0.22, 0.18) * values
    return jnp.clip(values, min=-most, max=most).astype(kind)


def setup_inputs(seed: int = 0) -> dict:
    splits = jax.random.split(jax.random.key(seed), 7)
    queries = draw_queries(jax.random.fold_in(splits[6], 71), 0)
    keys = draw_keys(jax.random.fold_in(splits[6], 71), 0)
    values = noise(splits[2], (ROUNDS, N_SEQ * BLOCK, KV_HEADS * HEAD), 1.0, 6.0, ((1, 32), (2, 8)))
    selected = draw_selected(jax.random.fold_in(splits[6], 71), 0)
    length = jax.random.randint(splits[4], (1,), TOKENS // 2, TOKENS + 1).astype(jnp.int32)
    out_weight = noise(splits[5], (HEADS * HEAD, MODEL), (HEADS * HEAD) ** -0.5, 0.09375, ((0, 8),))
    return dict(queries=queries, keys=keys, values=values, selected=selected, length=length, out_weight=out_weight)


def tile_attention(query_tile, key_tile, value_tile, causal_mask):
    scores = jnp.dot(query_tile, key_tile.T, preferred_element_type=jnp.float32) * (HEAD ** -0.5)
    scores = jnp.where(causal_mask, scores, -1e30)
    row_max = jnp.max(scores, axis=-1)
    weights = jnp.exp(scores - row_max[:, None])
    row_sum = jnp.sum(weights, axis=-1)
    mixed_rows = jnp.dot(weights.astype(jnp.bfloat16), value_tile, preferred_element_type=jnp.float32)
    return (mixed_rows / row_sum[:, None]).astype(jnp.bfloat16), row_max, row_sum


def merge_parts(own_u, own_m, own_l, far_u, far_m, far_l, usable):
    usable_rows = usable[:, :, None]
    far_safe = jnp.where(usable_rows, far_m, own_m[:, None, :])
    highest = jnp.maximum(own_m, jnp.max(far_safe, axis=1))
    own_weight = own_l * jnp.exp(own_m - highest)
    far_weight = jnp.where(usable_rows, far_l * jnp.exp(far_safe - highest[:, None, :]), jnp.float32(0.0))
    weighted = own_weight[..., None] * own_u.astype(jnp.float32)
    weighted = weighted + jnp.sum(far_weight[..., None] * far_u.astype(jnp.float32), axis=1)
    return weighted / (own_weight + jnp.sum(far_weight, axis=1))[..., None]


def reference(queries, keys, values, selected, length, out_weight):
    group_size = HEADS // KV_HEADS
    block_total = ROUNDS * N_SEQ
    query_blocks = queries.reshape(block_total, BLOCK, HEADS, HEAD).transpose(0, 2, 1, 3)
    key_blocks = keys.reshape(block_total, BLOCK, KV_HEADS, HEAD).transpose(0, 2, 1, 3)
    value_blocks = values.reshape(block_total, BLOCK, KV_HEADS, HEAD).transpose(0, 2, 1, 3)
    chosen_all = selected.reshape(block_total, HEADS, TOPK)
    head_kv = jnp.arange(HEADS, dtype=jnp.int32) // group_size
    causal = lax.broadcasted_iota(jnp.int32, (BLOCK, BLOCK), 0) >= lax.broadcasted_iota(jnp.int32, (BLOCK, BLOCK), 1)
    own_map = jax.vmap(tile_attention, in_axes=(0, 0, 0, None))
    far_map = jax.vmap(jax.vmap(tile_attention, in_axes=(None, 0, 0, None)), in_axes=(0, 0, 0, None))

    def one_block(block_index):
        block_q = query_blocks[block_index]
        own_u, own_m, own_l = own_map(block_q, key_blocks[block_index][head_kv], value_blocks[block_index][head_kv], causal)
        chosen = chosen_all[block_index]
        usable = chosen < block_index
        far_k = key_blocks[chosen, head_kv[:, None]]
        far_v = value_blocks[chosen, head_kv[:, None]]
        far_u, far_m, far_l = far_map(block_q, far_k, far_v, True)
        merged = merge_parts(own_u, own_m, own_l, far_u, far_m, far_l, usable)
        positions = block_index * BLOCK + jnp.arange(BLOCK, dtype=jnp.int32)
        live_rows = positions < length[0]
        merged = jnp.where(live_rows[None, :, None], merged, jnp.float32(0.0)).astype(jnp.bfloat16)
        return merged.transpose(1, 0, 2).reshape(BLOCK, HEADS * HEAD)

    attended = lax.map(one_block, jnp.arange(block_total, dtype=jnp.int32))
    attended = attended.reshape(ROUNDS, N_SEQ * BLOCK, HEADS * HEAD)
    group_width = HEADS * HEAD // N_HEAD

    def project_round(row_block):
        running_sum = jnp.zeros((row_block.shape[0], MODEL), jnp.float32)
        for member in range(N_HEAD):
            low = member * group_width
            group_term = jnp.dot(row_block[:, low:low + group_width], out_weight[low:low + group_width], preferred_element_type=jnp.float32).astype(jnp.bfloat16)
            group_term = lax.optimization_barrier(group_term)
            running_sum = running_sum + group_term.astype(jnp.float32)
        return running_sum.astype(jnp.bfloat16)

    projected = lax.map(project_round, attended)
    return attended, projected
```

```python
import functools

import jax
import jax.numpy as jnp
from jax import lax
from jax.experimental import pallas as pl
from jax.experimental.pallas import tpu as pltpu
from jax.sharding import PartitionSpec as P

HEAD = 128
SCALE = HEAD ** (-0.5)
LOG2E = 1.4426950408889634


def tile_scores(key_tile, query_tile):
    return lax.dot_general(
        key_tile, query_tile, (((1,), (1,)), ((), ())), preferred_element_type=jnp.float32
    )


def attention_kernel(
    top_count, block_of, usable_of, live, q_ref, k_ref, v_ref, fk_ref, fv_ref, o_ref, top, total, acc
):
    head = pl.program_id(0)
    slot = pl.program_id(1)
    block_len = q_ref.shape[0]

    @pl.when(slot == 0)
    def _():
        scores = tile_scores(k_ref[...], q_ref[...])
        key_at = lax.broadcasted_iota(jnp.int32, scores.shape, 0)
        query_at = lax.broadcasted_iota(jnp.int32, scores.shape, 1)
        scores = jnp.where(key_at <= query_at, scores, -1e30)
        highest = jnp.max(scores, axis=0, keepdims=True)
        weights = jnp.exp2((scores - highest) * (SCALE * LOG2E))
        top[...] = highest
        total[...] = jnp.sum(weights, axis=0, keepdims=True)
        acc[...] = lax.dot_general(
            v_ref[...],
            weights.astype(jnp.bfloat16),
            (((0,), (0,)), ((), ())),
            preferred_element_type=jnp.float32,
        )

    @pl.when(usable_of[head * top_count + slot] != 0)
    def _():
        scores = tile_scores(fk_ref[0, 0], q_ref[...])
        before = top[...]
        highest = jnp.maximum(before, jnp.max(scores, axis=0, keepdims=True))
        shrink = jnp.exp2((before - highest) * (SCALE * LOG2E))
        weights = jnp.exp2((scores - highest) * (SCALE * LOG2E))
        top[...] = highest
        total[...] = total[...] * shrink + jnp.sum(weights, axis=0, keepdims=True)
        acc[...] = acc[...] * shrink + lax.dot_general(
            fv_ref[0, 0],
            weights.astype(jnp.bfloat16),
            (((0,), (0,)), ((), ())),
            preferred_element_type=jnp.float32,
        )

    @pl.when(slot == top_count - 1)
    def _():
        rows = lax.broadcasted_iota(jnp.int32, (1, block_len), 1)
        mixed = jnp.where(rows < live[0], acc[...] / total[...], 0.0)
        o_ref[...] = mixed.T.astype(jnp.bfloat16)


def attend(queries, keys, values, far, round_now, chosen, usable, live):
    block_len, row_width = queries.shape
    heads = row_width // HEAD
    top_count = chosen.shape[1]
    members = far.shape[1] // 2
    chosen = chosen.reshape(-1)

    def far_map(part, head, slot, block_of, usable_of, live):
        block = block_of[head * top_count + slot]
        return (block % 32, block // 32 * 2 + part, 0, 0)

    return pl.pallas_call(
        functools.partial(attention_kernel, top_count),
        grid_spec=pltpu.PrefetchScalarGridSpec(
            num_scalar_prefetch=3,
            grid=(heads, top_count),
            in_specs=[
                pl.BlockSpec((block_len, HEAD), lambda h, j, *_: (0, h)),
                pl.BlockSpec((block_len, HEAD), lambda h, j, *_: (0, 0)),
                pl.BlockSpec((block_len, HEAD), lambda h, j, *_: (0, 0)),
                pl.BlockSpec((1, 1, block_len, HEAD), functools.partial(far_map, 0)),
                pl.BlockSpec((1, 1, block_len, HEAD), functools.partial(far_map, 1)),
            ],
            out_specs=pl.BlockSpec((block_len, HEAD), lambda h, j, *_: (0, h)),
            scratch_shapes=[
                pltpu.VMEM((1, block_len), jnp.float32),
                pltpu.VMEM((1, block_len), jnp.float32),
                pltpu.VMEM((HEAD, block_len), jnp.float32),
            ],
        ),
        out_shape=jax.ShapeDtypeStruct((block_len, row_width), jnp.bfloat16),
        compiler_params=pltpu.CompilerParams(vmem_limit_bytes=32 * 1024 * 1024),
        cost_estimate=pl.CostEstimate(
            flops=16 * 4 * block_len * block_len * HEAD * 2,
            bytes_accessed=12 * 1024 * 1024,
            transcendentals=16 * block_len * block_len,
        ),
        name=f"attend_{round_now}",
    )(chosen, usable, live, queries, keys, values, far, far)


def per_device(queries, keys, values, selected, length, out_weight):
    rounds, block_len, row_width = queries.shape
    peers = lax.axis_size("seq")
    my_seq = lax.axis_index("seq")
    gathered = [
        lax.all_gather(jnp.stack([keys[r], values[r]]), "seq", axis=0) for r in range(rounds)
    ]
    attended, projected = [], []
    for r in range(rounds):
        block = r * peers + my_seq
        chosen = selected[r, 0]
        usable = (chosen < block).astype(jnp.int32)
        safe = jnp.where(chosen < block, chosen, 0)
        far = gathered[0] if r == 0 else jnp.concatenate(gathered[: r + 1], axis=1)
        live = jnp.reshape(length[0] - block * block_len, (1,))
        rows = attend(
            queries[r], keys[r], values[r], far, r, safe, usable.reshape(-1), live
        )
        attended.append(rows)
        term = jnp.dot(rows, out_weight, preferred_element_type=jnp.float32).astype(jnp.bfloat16)
        projected.append(lax.psum_scatter(term, "head", scatter_dimension=0, tiled=True))
    return jnp.stack(attended), jnp.stack(projected)


def solution(mesh):
    placed = (
        P(None, "seq", "head"),
        P(None, "seq", "head"),
        P(None, "seq", "head"),
        P(None, "seq", "head", None),
        P(),
        P("head", None),
    )
    return jax.shard_map(
        per_device,
        mesh=mesh,
        in_specs=placed,
        out_specs=(P(None, "seq", "head"), P(None, ("seq", "head"), None)),
        check_vma=False,
    )
```

```python
import jax
import jax.numpy as jnp
from jax import lax
from jax.experimental import pallas as pl
from jax.experimental.pallas import tpu as pltpu
from jax.sharding import PartitionSpec as P

HEAD = 128
Z, X, Y = 8, 4, 4
PEERS = Z * X
BLOCK = 512
HEADS = 4
TOPK = 3
ROUNDS = 2
MODEL = 4096
GAIN = HEAD ** (-0.5) * 1.4426950408889634
CUT = 304
STAGES = 10
COMPUTE_END = (STAGES + 1) * 5 - 1
POST_0 = 34
POST_1 = COMPUTE_END
POST_STEPS = 12
COLS = 1024
HALF = COLS // 2
MESH = pl.DeviceIdType.MESH


def soft_part(key_tile, value_t, query_t, mask_from=None):
    scores = jnp.dot(key_tile, query_t, preferred_element_type=jnp.float32)
    if mask_from is not None:
        key_at = lax.broadcasted_iota(jnp.int32, scores.shape, 0)
        query_at = lax.broadcasted_iota(jnp.int32, scores.shape, 1) + mask_from
        scores = jnp.where(key_at <= query_at, scores, -1e30)
    highest = jnp.max(scores, axis=0, keepdims=True)
    weights = jnp.exp2((scores - highest) * GAIN)
    total = jnp.sum(weights, axis=0, keepdims=True)
    mixed = jnp.dot(value_t, weights.astype(jnp.bfloat16), preferred_element_type=jnp.float32)
    return mixed, highest, total


def value_rows(stacked):
    return jnp.concatenate([stacked[c * HEAD : (c + 1) * HEAD] for c in range(4)], axis=1)


def kernel(
    sel_ref, len_ref, q_ref, k_ref, v_ref, w_ref,
    att_ref, out_ref,
    kv, qt, us, ms, ls, wo, ws, sib, part, relay, fin, tile_of, round_of,
    ra, rb, saz, sax, sbx, sbz, wsem, att_s, att_r, rs_s, relay_r, fin_r,
):
    seq = lax.axis_index("seq")
    head = lax.axis_index("head")
    z, x = seq // X, lax.rem(seq, X)
    y, core = head // 2, lax.rem(head, 2)

    def at(zz, xx):
        return lax.rem(zz + 2 * Z, Z) * X + lax.rem(xx + 2 * X, X)

    up, down = at(z + 1, x), at(z - 1, x)
    right, left = at(z, x + 1), at(z, x - 1)
    front = lax.rem(y + 1, Y) * 2 + core
    back = lax.rem(y + 3, Y) * 2 + core
    twin = y * 2 + 1 - core

    barrier = pltpu.get_barrier_semaphore()
    for peer in (up, down, right, left):
        pl.semaphore_signal(barrier, inc=1, device_id={"seq": peer}, device_id_type=MESH)
    for peer in (front, back, twin):
        pl.semaphore_signal(barrier, inc=1, device_id={"head": peer}, device_id_type=MESH)

    for r in range(ROUNDS):
        kv[r, seq, 0] = k_ref[r]
        for c in range(4):
            rows = slice(c * HEAD, (c + 1) * HEAD)
            kv[r, seq, 1, rows, :] = v_ref[r, rows, :].T

    pl.semaphore_wait(barrier, 7)

    def copy_a(r, block, peer, send):
        view = kv.at[r, block, :, pl.ds(0, CUT), :]
        return pltpu.make_async_remote_copy(
            src_ref=view, dst_ref=view, send_sem=send, recv_sem=ra.at[r, block],
            device_id={"seq": peer}, device_id_type=MESH,
        )

    def copy_b(r, block, peer, send):
        view = kv.at[r, block, :, pl.ds(CUT, BLOCK - CUT), :]
        return pltpu.make_async_remote_copy(
            src_ref=view, dst_ref=view, send_sem=send, recv_sem=rb.at[r, block],
            device_id={"seq": peer}, device_id_type=MESH,
        )

    def wait_a(r, block):
        copy_a(r, block, up, saz.at[r, 8]).wait_recv()

    def wait_b(r, block):
        copy_b(r, block, up, sbz.at[r, 32]).wait_recv()

    def launch(r, act):
        act(copy_b(r, seq, right, sbx.at[r, 0]))
        act(copy_b(r, seq, left, sbx.at[r, 1]))
        act(copy_a(r, seq, up, saz.at[r, z]))
        act(copy_a(r, seq, down, saz.at[r, 8]))
        act(copy_b(r, seq, up, sbz.at[r, seq]))
        act(copy_b(r, seq, down, sbz.at[r, 32 + x]))
        act(copy_a(r, seq, right, sax.at[r, z, 0]))
        act(copy_a(r, seq, left, sax.at[r, z, 1]))

    def below(r, k):
        return jnp.logical_or(
            jnp.logical_and(k == 0, r == 0), jnp.logical_and(k == Z // 2, r == 1)
        )

    def comm(r, k, i, act, waits):
        inner = jnp.logical_and(k > 0, k < Z // 2)
        lo_z, hi_z = lax.rem(z + Z - k, Z), lax.rem(z + k, Z)
        use_lo = jnp.logical_or(inner, below(r, k))
        use_hi = jnp.logical_or(inner, jnp.logical_not(below(r, k)))
        use_hi = jnp.logical_and(use_hi, jnp.logical_or(inner, jnp.logical_not(use_lo)))

        @pl.when(jnp.logical_and(i == 0, k > 0))
        def _():
            lo, hi = at(lo_z, x), at(hi_z, x)
            if waits:
                wait_a(r, lo)

            @pl.when(jnp.logical_or(k < 3, jnp.logical_and(k == 3, r == 0)))
            def _():
                act(copy_a(r, lo, up, saz.at[r, lo_z]))

            act(copy_a(r, lo, right, sax.at[r, lo_z, 0]))
            act(copy_a(r, lo, left, sax.at[r, lo_z, 1]))

            @pl.when(inner)
            def _():
                if waits:
                    wait_a(r, hi)

                @pl.when(jnp.logical_or(k < 3, r == 1))
                def _():
                    act(copy_a(r, hi, down, saz.at[r, hi_z]))

                act(copy_a(r, hi, right, sax.at[r, hi_z, 0]))
                act(copy_a(r, hi, left, sax.at[r, hi_z, 1]))

        @pl.when(i > 0)
        def _():
            off = jnp.where(i == 1, 0, jnp.where(i == 2, 1, jnp.where(i == 3, 3, 2)))
            col = lax.rem(x + off, X)
            lo, hi = at(lo_z, col), at(hi_z, col)

            @pl.when(jnp.logical_and(k == 0, i > 1))
            def _():
                if waits:
                    wait_b(r, lo)

                @pl.when(jnp.logical_and(i == 2, r == 1))
                def _():
                    act(copy_b(r, lo, left, sbx.at[r, 2]))

                @pl.when(jnp.logical_and(i == 3, r == 0))
                def _():
                    act(copy_b(r, lo, right, sbx.at[r, 2]))

                act(copy_b(r, lo, up, sbz.at[r, lo]))
                act(copy_b(r, lo, down, sbz.at[r, 32 + col]))

            @pl.when(k > 0)
            def _():
                if waits:
                    wait_b(r, lo)

                @pl.when(jnp.logical_or(k < 3, jnp.logical_and(k == 3, lax.rem(col, 2) == 0)))
                def _():
                    act(copy_b(r, lo, up, sbz.at[r, lo]))

                @pl.when(inner)
                def _():
                    if waits:
                        wait_b(r, hi)

                    @pl.when(jnp.logical_or(k < 3, lax.rem(col, 2) == 1))
                    def _():
                        act(copy_b(r, hi, down, sbz.at[r, hi]))

        @pl.when(jnp.logical_and(i == 3, use_lo))
        def _():
            block = at(lo_z, x - 1)
            if waits:
                wait_a(r, block)
            act(copy_a(r, block, right, sax.at[r, lo_z, 2]))

        @pl.when(jnp.logical_and(i == 3, use_hi))
        def _():
            block = at(hi_z, x + 1)
            if waits:
                wait_a(r, block)
            act(copy_a(r, block, left, sax.at[r, hi_z, 2]))

    def far_tile(r, block):
        query_t = qt.at[tile_of[block]]
        newer = round_of[block] == 1
        key_tile = jnp.where(newer, kv[r, block, 0], kv[0, block, 0])
        value_t = value_rows(jnp.where(newer, kv[r, block, 1], kv[0, block, 1]))
        for c in range(2):
            cols = slice(c * 256, (c + 1) * 256)
            mixed, highest, total = soft_part(key_tile, value_t, query_t[:, cols])
            us[block, :, cols] = mixed
            ms[block, :, cols] = highest
            ls[block, :, cols] = total

    def own_tile(tile, carry):
        r, h = tile // HEADS, lax.rem(tile, HEADS)
        query_t = q_ref[r, :, pl.ds(pl.multiple_of(h * HEAD, HEAD), HEAD)].T
        qt[tile] = query_t
        key_tile = kv[r, seq, 0]
        value_t = value_rows(kv[r, seq, 1])
        for c in range(2):
            cols = slice(c * 256, (c + 1) * 256)
            keys_to = (c + 1) * 256
            mixed, highest, total = soft_part(
                key_tile[:keys_to], value_t[:, :keys_to], query_t[:, cols], c * 256
            )
            us[PEERS + tile, :, cols] = mixed
            ms[PEERS + tile, :, cols] = highest
            ls[PEERS + tile, :, cols] = total
        return carry

    def compute(r, k, i):
        off = jnp.where(i == 0, 0, jnp.where(i == 1, 1, jnp.where(i == 2, 3, 2)))
        inner = jnp.logical_and(k > 0, k < Z // 2)

        def one(side, carry):
            zz = jnp.where(side == 0, z + Z - k, z + k)
            block = at(zz, x + off)
            is_below = jnp.where(inner, side == 0, below(r, k))
            live = jnp.logical_or(side == 0, inner)
            pending = jnp.logical_or(
                off == 2,
                jnp.logical_or(
                    jnp.logical_and(is_below, off == 1),
                    jnp.logical_and(jnp.logical_not(is_below), off == 3),
                ),
            )

            @pl.when(jnp.logical_and(live, pending))
            def _():
                wait_a(r, block)

            @pl.when(jnp.logical_and(live, jnp.logical_or(r == 0, block < seq)))
            def _():
                far_tile(r, block)

            return carry

        lax.fori_loop(0, 2, one, 0)

    def merge(r, h):
        tile = r * HEADS + h
        own = PEERS + tile
        slots, oks = [], []
        top = ms[own]
        for j in range(TOPK):
            chosen = sel_ref[r, 0, h, j]
            ok = chosen < r * PEERS + seq
            slot = jnp.where(ok, lax.rem(chosen, PEERS), 0)
            slots.append(slot)
            oks.append(ok)
            top = jnp.maximum(top, jnp.where(ok, ms[slot], top))
        weights = [jnp.exp2((ms[own] - top) * GAIN)]
        whole = weights[0] * ls[own]
        for slot, ok in zip(slots, oks):
            weight = jnp.where(ok, jnp.exp2(jnp.minimum(ms[slot] - top, 0.0) * GAIN), 0.0)
            weights.append(weight)
            whole = whole + weight * ls[slot]
        row = lax.broadcasted_iota(jnp.int32, (1, BLOCK), 1)
        alive = row < len_ref[0] - (r * PEERS + seq) * BLOCK
        norm = jnp.where(alive, 1.0 / whole, 0.0)
        mixed = us[own] * (weights[0] * norm)
        for slot, weight in zip(slots, weights[1:]):
            mixed = mixed + us[slot] * (weight * norm)
        rows = mixed.T.astype(jnp.bfloat16).reshape(Y, 2, 64, HEAD)
        att_ref[r, :, :, :, pl.ds(pl.multiple_of(h * HEAD, HEAD), HEAD)] = rows

    def copy_att(r):
        return pltpu.make_async_remote_copy(
            src_ref=att_ref.at[r, :, 1 - core], dst_ref=sib.at[r],
            send_sem=att_s.at[r], recv_sem=att_r.at[r],
            device_id={"head": twin}, device_id_type=MESH,
        )

    def copy_w():
        return pltpu.make_async_remote_copy(
            src_ref=w_ref, dst_ref=ws, send_sem=wsem.at[0], recv_sem=wsem.at[1],
            device_id={"head": twin}, device_id_type=MESH,
        )

    def load_w():
        return pltpu.make_async_copy(w_ref, wo, wsem.at[2])

    y_across, y_front, y_back = lax.rem(y + 2, Y), lax.rem(y + 1, Y), lax.rem(y + 3, Y)

    def copy_relay(r, n, side):
        return pltpu.make_async_remote_copy(
            src_ref=part.at[r, n, y_across, side], dst_ref=relay.at[r, n, side],
            send_sem=rs_s.at[r, n, side], recv_sem=relay_r.at[r, n, side],
            device_id={"head": front if side == 0 else back}, device_id_type=MESH,
        )

    def copy_fin(r, n, side, half):
        return pltpu.make_async_remote_copy(
            src_ref=part.at[r, n, y_front if side == 0 else y_back, half],
            dst_ref=fin.at[r, n, side, half],
            send_sem=rs_s.at[r, n, 2 + side * 2 + half], recv_sem=fin_r.at[r, n, side, half],
            device_id={"head": front if side == 0 else back}, device_id_type=MESH,
        )

    def project(r, n):
        own_rows = att_ref[r, :, core].reshape(Y * 64, HEADS * HEAD)
        twin_rows = sib[r].reshape(Y * 64, HEADS * HEAD)
        for half in range(2):
            cols = pl.ds(pl.multiple_of(n * COLS + half * HALF, HALF), HALF)
            term = jnp.dot(own_rows, wo[:, cols], preferred_element_type=jnp.float32)
            term = term + jnp.dot(twin_rows, ws[:, cols], preferred_element_type=jnp.float32)
            part[r, n, :, half] = term.astype(jnp.bfloat16).reshape(Y, 64, HALF)
        copy_relay(r, n, 0).start()
        copy_relay(r, n, 1).start()
        copy_fin(r, n, 0, 1).start()
        copy_fin(r, n, 1, 0).start()

    def pass_on(r, n):
        for side, target, half in ((0, y_front, 0), (1, y_back, 1)):
            copy_relay(r, n, side).wait_recv()
            total = part[r, n, target, half].astype(jnp.float32)
            total = total + relay[r, n, side].astype(jnp.float32)
            part[r, n, target, half] = total.astype(jnp.bfloat16)
            copy_fin(r, n, side, half).start()

    def finish(r, n):
        for side in range(2):
            for half in range(2):
                copy_fin(r, n, side, half).wait_recv()
        for half in range(2):
            total = part[r, n, y, half].astype(jnp.float32)
            total = total + fin[r, n, 0, half].astype(jnp.float32)
            total = total + fin[r, n, 1, half].astype(jnp.float32)
            cols = pl.ds(pl.multiple_of(n * COLS + half * HALF, HALF), HALF)
            out_ref[r, :, cols] = total.astype(jnp.bfloat16)

    def post(r, p):
        @pl.when(p < 4)
        def _():
            merge(r, p)

        @pl.when(p == 3)
        def _():
            copy_att(r).start()

        @pl.when(p == 4)
        def _():
            copy_att(r).wait_recv()

        @pl.when(jnp.logical_and(p == 4, r == 0))
        def _():
            load_w().wait()
            copy_w().wait_recv()

        @pl.when(jnp.logical_and(p >= 4, p < 8))
        def _():
            project(r, p - 4)

        @pl.when(jnp.logical_and(p >= 6, p < 10))
        def _():
            pass_on(r, p - 6)

        @pl.when(p >= 8)
        def _():
            finish(r, p - 8)

    def stage_of(g):
        r = jnp.where(jnp.logical_or(g == 4, g > 5), 1, 0)
        k = jnp.where(g < 4, g, jnp.where(g == 4, 0, jnp.where(g == 5, 4, g - 5)))
        return r, k

    start = lambda copy: copy.start()
    drain = lambda copy: copy.wait_send()

    launch(0, start)
    load_w().start()
    copy_w().start()

    def table(block, carry):
        tile, newer = jnp.int32(0), jnp.int32(0)
        for r in range(ROUNDS):
            for h in range(HEADS):
                for j in range(TOPK):
                    chosen = sel_ref[r, 0, h, j]
                    hit = jnp.logical_and(
                        lax.rem(chosen, PEERS) == block, chosen < r * PEERS + seq
                    )
                    tile = jnp.where(hit, r * HEADS + h, tile)
                    newer = jnp.where(hit, chosen // PEERS, newer)
        tile_of[block] = tile
        round_of[block] = newer
        return carry

    lax.fori_loop(0, ROUNDS * HEADS, own_tile, 0)
    lax.fori_loop(0, PEERS, table, 0)

    def step(t, carry):
        g, i = t // 5, lax.rem(t, 5)

        @pl.when(g < STAGES)
        def _():
            r, k = stage_of(g)
            comm(r, k, i, start, True)

        @pl.when(t == 19)
        def _():
            launch(1, start)

        @pl.when(jnp.logical_and(jnp.logical_and(g > 0, i < 4), t < COMPUTE_END))
        def _():
            r, k = stage_of(g - 1)
            compute(r, k, i)

        late = t >= POST_1
        p = t - jnp.where(late, POST_1, POST_0)

        @pl.when(jnp.logical_and(p >= 0, p < POST_STEPS))
        def _():
            post(jnp.where(late, 1, 0), p)

        return carry

    lax.fori_loop(0, POST_1 + POST_STEPS, step, 0)

    def drain_step(t, carry):
        r, k = stage_of(t // 5)
        comm(r, k, lax.rem(t, 5), drain, False)
        return carry

    launch(0, drain)
    launch(1, drain)
    lax.fori_loop(0, STAGES * 5, drain_step, 0)
    copy_w().wait_send()
    for r in range(ROUNDS):
        copy_att(r).wait_send()

        def drain_sum(n, carry, r=r):
            for side in range(2):
                copy_relay(r, n, side).wait_send()
                for half in range(2):
                    copy_fin(r, n, side, half).wait_send()
            return carry

        lax.fori_loop(0, MODEL // COLS, drain_sum, 0)


def per_device(queries, keys, values, selected, length, out_weight):
    vmem = pl.BlockSpec(memory_space=pltpu.VMEM)
    smem = pl.BlockSpec(memory_space=pltpu.SMEM)
    bf16, f32 = jnp.bfloat16, jnp.float32
    tiles = MODEL // COLS
    dma = pltpu.SemaphoreType.DMA
    attended, projected = pl.pallas_call(
        kernel,
        out_shape=(
            jax.ShapeDtypeStruct((ROUNDS, Y, 2, 64, HEADS * HEAD), bf16),
            jax.ShapeDtypeStruct((ROUNDS, 64, MODEL), bf16),
        ),
        in_specs=[smem, smem, vmem, vmem, vmem, pl.BlockSpec(memory_space=pl.ANY)],
        out_specs=(vmem, vmem),
        scratch_shapes=[
            pltpu.VMEM((ROUNDS, PEERS, 2, BLOCK, HEAD), bf16),
            pltpu.VMEM((ROUNDS * HEADS, HEAD, BLOCK), bf16),
            pltpu.VMEM((PEERS + ROUNDS * HEADS, HEAD, BLOCK), f32),
            pltpu.VMEM((PEERS + ROUNDS * HEADS, 1, BLOCK), f32),
            pltpu.VMEM((PEERS + ROUNDS * HEADS, 1, BLOCK), f32),
            pltpu.VMEM((HEADS * HEAD, MODEL), bf16),
            pltpu.VMEM((HEADS * HEAD, MODEL), bf16),
            pltpu.VMEM((ROUNDS, Y, 64, HEADS * HEAD), bf16),
            pltpu.VMEM((ROUNDS, tiles, Y, 2, 64, HALF), bf16),
            pltpu.VMEM((ROUNDS, tiles, 2, 64, HALF), bf16),
            pltpu.VMEM((ROUNDS, tiles, 2, 2, 64, HALF), bf16),
            pltpu.SMEM((PEERS,), jnp.int32),
            pltpu.SMEM((PEERS,), jnp.int32),
            dma((ROUNDS, PEERS)),
            dma((ROUNDS, PEERS)),
            dma((ROUNDS, Z + 1)),
            dma((ROUNDS, Z, 3)),
            dma((ROUNDS, 3)),
            dma((ROUNDS, PEERS + X)),
            dma((3,)),
            dma((ROUNDS,)),
            dma((ROUNDS,)),
            dma((ROUNDS, tiles, 6)),
            dma((ROUNDS, tiles, 2)),
            dma((ROUNDS, tiles, 2, 2)),
        ],
        compiler_params=pltpu.CompilerParams(
            collective_id=0, has_side_effects=True, vmem_limit_bytes=60 * 1024 * 1024
        ),
        cost_estimate=pl.CostEstimate(
            flops=72 * 4 * BLOCK * BLOCK * HEAD, bytes_accessed=8 * 1024 * 1024, transcendentals=72 * BLOCK * BLOCK
        ),
        name="attend_and_project",
    )(selected, length, queries, keys, values, out_weight)
    return attended.reshape(ROUNDS, BLOCK, HEADS * HEAD), projected


def solution(mesh):
    placed = (
        P(None, "seq", "head"),
        P(None, "seq", "head"),
        P(None, "seq", "head"),
        P(None, "seq", "head", None),
        P(),
        P("head", None),
    )
    return jax.shard_map(
        per_device,
        mesh=mesh,
        in_specs=placed,
        out_specs=(P(None, "seq", "head"), P(None, ("seq", "head"), None)),
        check_vma=False,
    )
```

```python
import jax
import jax.numpy as jnp
from jax import lax
from jax.experimental import pallas as pl
from jax.experimental.pallas import tpu as pltpu
from jax.sharding import PartitionSpec as P

HEAD = 128
Z, X, Y = 8, 4, 4
PEERS = Z * X
BLOCK = 512
HEADS = 4
TOPK = 3
ROUNDS = 2
MODEL = 4096
GAIN = HEAD ** (-0.5) * 1.4426950408889634
CUT = 304
COLS = 1024
HALF = COLS // 2
TILES = MODEL // COLS
MESH = pl.DeviceIdType.MESH
STEPS = 102
FORWARD = (
    5179011, 524288, 17, 67895296, 206483, 4718627, 33, 109922067,
    12862515, 149171, 17065395, 3245635, 3565507, 66, 84677657, 7149451,
    0, 107762176, 79360, 14955563, 218891, 44826624, 19166720, 116274730,
    95744, 19437056, 120354091, 161483, 331, 0, 0, 0,
    0, 0,
)
WORK = (
    4718592, 1025, 13173257, 4474241, 67384320, 29738, 38216225, 139776,
    12927488, 109462016, 46399498, 17039793, 0, 117801777, 0, 103092736,
    5145113, 9175043, 5244979, 13631524, 69478917, 107235993, 1600041, 5984937,
    14969894, 37657, 115700224, 52843465, 3044169, 15488539, 11548684, 7632909,
    16013838, 16276510,
)


def soft_part(key_tile, value_t, query_t, mask_from=None):
    scores = jnp.dot(key_tile, query_t, preferred_element_type=jnp.float32)
    if mask_from is not None:
        key_at = lax.broadcasted_iota(jnp.int32, scores.shape, 0)
        query_at = lax.broadcasted_iota(jnp.int32, scores.shape, 1) + mask_from
        scores = jnp.where(key_at <= query_at, scores, -1e30)
    highest = jnp.max(scores, axis=0, keepdims=True)
    weights = jnp.exp2((scores - highest) * GAIN)
    total = jnp.sum(weights, axis=0, keepdims=True)
    mixed = jnp.dot(value_t, weights.astype(jnp.bfloat16), preferred_element_type=jnp.float32)
    return mixed, highest, total


def value_rows(stacked):
    return jnp.concatenate([stacked[c * HEAD : (c + 1) * HEAD] for c in range(4)], axis=1)


def kernel(
    sel_ref, len_ref, q_ref, k_ref, v_ref, w_ref,
    att_ref, out_ref,
    kv, qv, vv, qt, us, ms, ls, wo, ws, attx, sib, part, relay, fin, outv, tile_of, round_of,
    ra, rb, saz, sax, sbx, sbz, insem, wsem, att_s, att_r, rs_s, relay_r, fin_r, att_o, out_o,
):
    seq = lax.axis_index("seq")
    head = lax.axis_index("head")
    z, x = seq // X, lax.rem(seq, X)
    y, core = head // 2, lax.rem(head, 2)

    def at(zz, xx):
        return lax.rem(zz + 2 * Z, Z) * X + lax.rem(xx + 2 * X, X)

    up, down = at(z + 1, x), at(z - 1, x)
    right, left = at(z, x + 1), at(z, x - 1)
    front = lax.rem(y + 1, Y) * 2 + core
    back = lax.rem(y + 3, Y) * 2 + core
    twin = y * 2 + 1 - core

    barrier = pltpu.get_barrier_semaphore()
    for peer in (up, down, right, left):
        pl.semaphore_signal(barrier, inc=1, device_id={"seq": peer}, device_id_type=MESH)
    for peer in (front, back, twin):
        pl.semaphore_signal(barrier, inc=1, device_id={"head": peer}, device_id_type=MESH)

    load_v = pltpu.make_async_copy(v_ref, vv, insem.at[0])
    load_k = [
        pltpu.make_async_copy(k_ref.at[r], kv.at[r, seq, 0], insem.at[1 + r]) for r in range(ROUNDS)
    ]
    load_q = pltpu.make_async_copy(q_ref, qv, insem.at[3])
    load_w = pltpu.make_async_copy(w_ref, wo, wsem.at[2])
    load_v.start()
    for load in load_k:
        load.start()
    load_q.start()
    load_v.wait()
    for r in range(ROUNDS):
        for c in range(4):
            rows = slice(c * HEAD, (c + 1) * HEAD)
            kv[r, seq, 1, rows, :] = vv[r, rows, :].T
    for load in load_k:
        load.wait()
    pl.semaphore_wait(barrier, 7)

    def copy_a(r, block, peer, send):
        view = kv.at[r, block, :, pl.ds(0, CUT), :]
        return pltpu.make_async_remote_copy(
            src_ref=view, dst_ref=view, send_sem=send, recv_sem=ra.at[r, block],
            device_id={"seq": peer}, device_id_type=MESH,
        )

    def copy_b(r, block, peer, send):
        view = kv.at[r, block, :, pl.ds(CUT, BLOCK - CUT), :]
        return pltpu.make_async_remote_copy(
            src_ref=view, dst_ref=view, send_sem=send, recv_sem=rb.at[r, block],
            device_id={"seq": peer}, device_id_type=MESH,
        )

    def wait_a(r, block):
        copy_a(r, block, up, saz.at[r, 8]).wait_recv()

    def wait_b(r, block):
        copy_b(r, block, up, sbz.at[r, 32]).wait_recv()

    def launch_b(r, act):
        act(copy_b(r, seq, right, sbx.at[r, 0]))
        act(copy_b(r, seq, left, sbx.at[r, 1]))
        act(copy_b(r, seq, up, sbz.at[r, seq]))
        act(copy_b(r, seq, down, sbz.at[r, 32 + x]))

    def launch_a(r, act):
        act(copy_a(r, seq, up, saz.at[r, z]))
        act(copy_a(r, seq, down, saz.at[r, 8]))
        act(copy_a(r, seq, right, sax.at[r, z, 0]))
        act(copy_a(r, seq, left, sax.at[r, z, 1]))

    def inner_of(k):
        return jnp.logical_and(k > 0, k < Z // 2)

    def below(r, k):
        return jnp.logical_or(
            jnp.logical_and(k == 0, r == 0), jnp.logical_and(k == Z // 2, r == 1)
        )

    def forward_a(r, k, act, waits):
        lo_z, hi_z = lax.rem(z + Z - k, Z), lax.rem(z + k, Z)
        lo, hi = at(lo_z, x), at(hi_z, x)
        if waits:
            wait_a(r, lo)

        @pl.when(jnp.logical_or(k < 3, jnp.logical_and(k == 3, r == 0)))
        def _():
            act(copy_a(r, lo, up, saz.at[r, lo_z]))

        act(copy_a(r, lo, right, sax.at[r, lo_z, 0]))
        act(copy_a(r, lo, left, sax.at[r, lo_z, 1]))

        @pl.when(k < 4)
        def _():
            if waits:
                wait_a(r, hi)

            @pl.when(jnp.logical_or(k < 3, r == 1))
            def _():
                act(copy_a(r, hi, down, saz.at[r, hi_z]))

            act(copy_a(r, hi, right, sax.at[r, hi_z, 0]))
            act(copy_a(r, hi, left, sax.at[r, hi_z, 1]))

    def forward_f(r, k, act, waits):
        lo_z, hi_z = lax.rem(z + Z - k, Z), lax.rem(z + k, Z)
        inner, is_below = inner_of(k), below(r, k)

        @pl.when(jnp.logical_or(inner, is_below))
        def _():
            block = at(lo_z, x - 1)
            if waits:
                wait_a(r, block)
            act(copy_a(r, block, right, sax.at[r, lo_z, 2]))

        @pl.when(jnp.logical_or(inner, jnp.logical_not(is_below)))
        def _():
            block = at(hi_z, x + 1)
            if waits:
                wait_a(r, block)
            act(copy_a(r, block, left, sax.at[r, hi_z, 2]))

    def forward_b(r, k, off, act, waits):
        lo_z, hi_z = lax.rem(z + Z - k, Z), lax.rem(z + k, Z)
        col = lax.rem(x + off, X)
        lo, hi = at(lo_z, col), at(hi_z, col)
        if waits:
            wait_b(r, lo)

        @pl.when(k == 0)
        def _():
            @pl.when(jnp.logical_and(off == 1, r == 1))
            def _():
                act(copy_b(r, lo, left, sbx.at[r, 2]))

            @pl.when(jnp.logical_and(off == 3, r == 0))
            def _():
                act(copy_b(r, lo, right, sbx.at[r, 2]))

            act(copy_b(r, lo, up, sbz.at[r, lo]))
            act(copy_b(r, lo, down, sbz.at[r, 32 + col]))

        @pl.when(k > 0)
        def _():
            @pl.when(jnp.logical_or(k < 3, jnp.logical_and(k == 3, lax.rem(col, 2) == 0)))
            def _():
                act(copy_b(r, lo, up, sbz.at[r, lo]))

            @pl.when(k < 4)
            def _():
                if waits:
                    wait_b(r, hi)

                @pl.when(jnp.logical_or(k < 3, lax.rem(col, 2) == 1))
                def _():
                    act(copy_b(r, hi, down, sbz.at[r, hi]))

    def far_tile(r, block):
        query_t = qt.at[tile_of[block]]
        newer = round_of[block] == 1
        key_tile = jnp.where(newer, kv[r, block, 0], kv[0, block, 0])
        value_t = value_rows(jnp.where(newer, kv[r, block, 1], kv[0, block, 1]))
        for c in range(2):
            cols = slice(c * 256, (c + 1) * 256)
            mixed, highest, total = soft_part(key_tile, value_t, query_t[:, cols])
            us[block, :, cols] = mixed
            ms[block, :, cols] = highest
            ls[block, :, cols] = total

    def own_tile(r, h):
        tile = r * HEADS + h
        key_tile = kv[r, seq, 0]
        value_t = value_rows(kv[r, seq, 1])
        for c in range(2):
            cols = slice(c * 256, (c + 1) * 256)
            keys_to = (c + 1) * 256
            mixed, highest, total = soft_part(
                key_tile[:keys_to], value_t[:, :keys_to], qt[tile, :, cols], c * 256
            )
            us[PEERS + tile, :, cols] = mixed
            ms[PEERS + tile, :, cols] = highest
            ls[PEERS + tile, :, cols] = total

    def far_slots(r, k, off):
        inner, is_below = inner_of(k), below(r, k)

        def one(side, carry):
            zz = jnp.where(side == 0, z + Z - k, z + k)
            block = at(zz, x + off)
            from_left = jnp.where(inner, side == 0, is_below)
            live = jnp.logical_or(side == 0, inner)
            pending = jnp.logical_or(
                off == 2,
                jnp.logical_or(
                    jnp.logical_and(from_left, off == 1),
                    jnp.logical_and(jnp.logical_not(from_left), off == 3),
                ),
            )

            @pl.when(jnp.logical_and(live, pending))
            def _():
                wait_a(r, block)

            @pl.when(jnp.logical_and(live, jnp.logical_or(r == 0, block < seq)))
            def _():
                far_tile(r, block)

            return carry

        lax.fori_loop(0, 2, one, 0)

    def copy_att(r, h):
        return pltpu.make_async_remote_copy(
            src_ref=attx.at[r, 1 - core, h], dst_ref=sib.at[r, h],
            send_sem=att_s.at[r, h], recv_sem=att_r.at[r, h],
            device_id={"head": twin}, device_id_type=MESH,
        )

    def store_att(r, h, c):
        cols = pl.ds(pl.multiple_of(h * HEAD, HEAD), HEAD)
        return pltpu.make_async_copy(
            attx.at[r, c, h], att_ref.at[r, :, c, :, cols], att_o.at[r, h, c]
        )

    def merge(r, h):
        tile = r * HEADS + h
        own = PEERS + tile
        slots, oks = [], []
        top = ms[own]
        for j in range(TOPK):
            chosen = sel_ref[r, j, 0, h]
            ok = chosen < r * PEERS + seq
            slot = jnp.where(ok, lax.rem(chosen, PEERS), 0)
            slots.append(slot)
            oks.append(ok)
            top = jnp.maximum(top, jnp.where(ok, ms[slot], top))
        weights = [jnp.exp2((ms[own] - top) * GAIN)]
        whole = weights[0] * ls[own]
        for slot, ok in zip(slots, oks):
            weight = jnp.where(ok, jnp.exp2(jnp.minimum(ms[slot] - top, 0.0) * GAIN), 0.0)
            weights.append(weight)
            whole = whole + weight * ls[slot]
        row = lax.broadcasted_iota(jnp.int32, (1, BLOCK), 1)
        alive = row < len_ref[0] - (r * PEERS + seq) * BLOCK
        norm = jnp.where(alive, 1.0 / whole, 0.0)
        mixed = us[own] * (weights[0] * norm)
        for slot, weight in zip(slots, weights[1:]):
            mixed = mixed + us[slot] * (weight * norm)
        rows = mixed.T.astype(jnp.bfloat16).reshape(Y, 2, 64, HEAD)
        for c in range(2):
            attx[r, c, h] = rows[:, c]
        copy_att(r, h).start()
        for c in range(2):
            store_att(r, h, c).start()

    def copy_w():
        return pltpu.make_async_remote_copy(
            src_ref=w_ref, dst_ref=ws, send_sem=wsem.at[0], recv_sem=wsem.at[1],
            device_id={"head": twin}, device_id_type=MESH,
        )

    y_across, y_front, y_back = lax.rem(y + 2, Y), lax.rem(y + 1, Y), lax.rem(y + 3, Y)

    def copy_relay(r, n, side):
        return pltpu.make_async_remote_copy(
            src_ref=part.at[r, n, y_across, side], dst_ref=relay.at[r, n, side],
            send_sem=rs_s.at[r, n, side], recv_sem=relay_r.at[r, n, side],
            device_id={"head": front if side == 0 else back}, device_id_type=MESH,
        )

    def copy_fin(r, n, side, half):
        return pltpu.make_async_remote_copy(
            src_ref=part.at[r, n, y_front if side == 0 else y_back, half],
            dst_ref=fin.at[r, n, side, half],
            send_sem=rs_s.at[r, n, 2 + side * 2 + half], recv_sem=fin_r.at[r, n, side, half],
            device_id={"head": front if side == 0 else back}, device_id_type=MESH,
        )

    def project(r, n):
        own_rows = jnp.concatenate(
            [attx[r, core, h].reshape(Y * 64, HEAD) for h in range(HEADS)], axis=1
        )
        twin_rows = jnp.concatenate(
            [sib[r, h].reshape(Y * 64, HEAD) for h in range(HEADS)], axis=1
        )
        for half in range(2):
            cols = pl.ds(pl.multiple_of(n * COLS + half * HALF, HALF), HALF)
            term = jnp.dot(own_rows, wo[:, cols], preferred_element_type=jnp.float32)
            term = term + jnp.dot(twin_rows, ws[:, cols], preferred_element_type=jnp.float32)
            part[r, n, :, half] = term.astype(jnp.bfloat16).reshape(Y, 64, HALF)
        copy_relay(r, n, 0).start()
        copy_relay(r, n, 1).start()
        copy_fin(r, n, 0, 1).start()
        copy_fin(r, n, 1, 0).start()

    def pass_on(r, n):
        for side, target, half in ((0, y_front, 0), (1, y_back, 1)):
            copy_relay(r, n, side).wait_recv()
            total = part[r, n, target, half].astype(jnp.float32)
            total = total + relay[r, n, side].astype(jnp.float32)
            part[r, n, target, half] = total.astype(jnp.bfloat16)
            copy_fin(r, n, side, half).start()

    def store_out(r, n):
        cols = pl.ds(pl.multiple_of(n * COLS, COLS), COLS)
        return pltpu.make_async_copy(outv.at[r, :, cols], out_ref.at[r, :, cols], out_o.at[r, n])

    def finish(r, n):
        for side in range(2):
            for half in range(2):
                copy_fin(r, n, side, half).wait_recv()
        for half in range(2):
            total = part[r, n, y, half].astype(jnp.float32)
            total = total + fin[r, n, 0, half].astype(jnp.float32)
            total = total + fin[r, n, 1, half].astype(jnp.float32)
            cols = pl.ds(pl.multiple_of(n * COLS + half * HALF, HALF), HALF)
            outv[r, :, cols] = total.astype(jnp.bfloat16)
        store_out(r, n).start()

    start = lambda copy: copy.start()
    drain = lambda copy: copy.wait_send()

    launch_b(0, start)
    launch_a(0, start)
    copy_w().start()
    load_w.start()

    def table(block, carry):
        tile, newer = jnp.int32(0), jnp.int32(0)
        for r in range(ROUNDS):
            for h in range(HEADS):
                for j in range(TOPK):
                    chosen = sel_ref[r, j, 0, h]
                    hit = jnp.logical_and(
                        lax.rem(chosen, PEERS) == block, chosen < r * PEERS + seq
                    )
                    tile = jnp.where(hit, r * HEADS + h, tile)
                    newer = jnp.where(hit, chosen // PEERS, newer)
        tile_of[block] = tile
        round_of[block] = newer
        return carry

    load_q.wait()
    for r in range(ROUNDS):
        for h in range(HEADS):
            qt[r * HEADS + h] = qv[r, :, h * HEAD : (h + 1) * HEAD].T
    lax.fori_loop(0, PEERS, table, 0)

    def step(t, carry):
        forward, work_code = jnp.int32(FORWARD[0]), jnp.int32(WORK[0])
        third = t // 3
        for w in range(1, len(FORWARD)):
            here = third == w
            forward = jnp.where(here, FORWARD[w], forward)
            work_code = jnp.where(here, WORK[w], work_code)
        bits = lax.rem(t, 3) * 9
        forward, work_code = forward >> bits, work_code >> bits
        kind, r, k, off = forward & 7, (forward >> 3) & 1, (forward >> 4) & 7, (forward >> 7) & 3

        @pl.when(kind == 1)
        def _():
            forward_a(r, k, start, True)

        @pl.when(kind == 2)
        def _():
            forward_f(r, k, start, True)

        @pl.when(kind == 3)
        def _():
            forward_b(r, k, off, start, True)

        @pl.when(kind == 4)
        def _():
            launch_a(1, start)

        @pl.when(kind == 5)
        def _():
            launch_b(1, start)

        work, wr = work_code & 7, (work_code >> 3) & 1
        item, woff = (work_code >> 4) & 7, (work_code >> 7) & 3

        @pl.when(work == 1)
        def _():
            far_slots(wr, item, woff)

        @pl.when(work == 2)
        def _():
            own_tile(wr, item)

        @pl.when(work == 3)
        def _():
            merge(wr, item)

        @pl.when(work == 4)
        def _():
            @pl.when(item == 0)
            def _():
                @pl.when(wr == 0)
                def _():
                    load_w.wait()
                    copy_w().wait_recv()

                for h in range(HEADS):
                    copy_att(wr, h).wait_recv()

            project(wr, item)

        @pl.when(work == 5)
        def _():
            pass_on(wr, item)

        @pl.when(work == 6)
        def _():
            finish(wr, item)

        return carry

    lax.fori_loop(0, STEPS, step, 0)

    def drain_step(t, carry):
        r, k, off = t // 20, lax.rem(t // 4, 5), lax.rem(t, 4)

        @pl.when(jnp.logical_or(k > 0, off > 0))
        def _():
            forward_b(r, k, off, drain, False)

        @pl.when(off == 0)
        def _():
            forward_f(r, k, drain, False)

        @pl.when(jnp.logical_and(off == 0, k > 0))
        def _():
            forward_a(r, k, drain, False)

        return carry

    for r in range(ROUNDS):
        launch_a(r, drain)
        launch_b(r, drain)
    lax.fori_loop(0, ROUNDS * 20, drain_step, 0)
    copy_w().wait_send()

    def drain_sum(t, carry):
        r, n = t // TILES, lax.rem(t, TILES)
        copy_att(r, n).wait_send()
        for c in range(2):
            store_att(r, n, c).wait()
        for side in range(2):
            copy_relay(r, n, side).wait_send()
            for half in range(2):
                copy_fin(r, n, side, half).wait_send()
        store_out(r, n).wait()
        return carry

    lax.fori_loop(0, ROUNDS * TILES, drain_sum, 0)


def hand_over(att_in, out_in, att_ref, out_ref, sems):
    copies = []
    for r in range(ROUNDS):
        for i in range(2):
            rows = slice(i * 256, (i + 1) * 256)
            copies.append((att_in.at[r, rows, :], att_ref.at[r, rows, :]))
            rows = slice(i * 32, (i + 1) * 32)
            copies.append((out_in.at[r, rows, :], out_ref.at[r, rows, :]))
    copies = [pltpu.make_async_copy(a, b, sems.at[i]) for i, (a, b) in enumerate(copies)]
    for copy in copies:
        copy.start()
    for copy in copies:
        copy.wait()


def per_device(queries, keys, values, selected, length, out_weight):
    anywhere = pl.BlockSpec(memory_space=pl.ANY)
    smem = pl.BlockSpec(memory_space=pltpu.SMEM)
    bf16, f32 = jnp.bfloat16, jnp.float32
    dma = pltpu.SemaphoreType.DMA
    attended, projected = pl.pallas_call(
        kernel,
        out_shape=(
            jax.ShapeDtypeStruct((ROUNDS, Y, 2, 64, HEADS * HEAD), bf16),
            jax.ShapeDtypeStruct((ROUNDS, 64, MODEL), bf16),
        ),
        in_specs=[smem, smem, anywhere, anywhere, anywhere, anywhere],
        out_specs=(anywhere, anywhere),
        scratch_shapes=[
            pltpu.VMEM((ROUNDS, PEERS, 2, BLOCK, HEAD), bf16),
            pltpu.VMEM((ROUNDS, BLOCK, HEADS * HEAD), bf16),
            pltpu.VMEM((ROUNDS, BLOCK, HEAD), bf16),
            pltpu.VMEM((ROUNDS * HEADS, HEAD, BLOCK), bf16),
            pltpu.VMEM((PEERS + ROUNDS * HEADS, HEAD, BLOCK), f32),
            pltpu.VMEM((PEERS + ROUNDS * HEADS, 1, BLOCK), f32),
            pltpu.VMEM((PEERS + ROUNDS * HEADS, 1, BLOCK), f32),
            pltpu.VMEM((HEADS * HEAD, MODEL), bf16),
            pltpu.VMEM((HEADS * HEAD, MODEL), bf16),
            pltpu.VMEM((ROUNDS, 2, HEADS, Y, 64, HEAD), bf16),
            pltpu.VMEM((ROUNDS, HEADS, Y, 64, HEAD), bf16),
            pltpu.VMEM((ROUNDS, TILES, Y, 2, 64, HALF), bf16),
            pltpu.VMEM((ROUNDS, TILES, 2, 64, HALF), bf16),
            pltpu.VMEM((ROUNDS, TILES, 2, 2, 64, HALF), bf16),
            pltpu.VMEM((ROUNDS, 64, MODEL), bf16),
            pltpu.SMEM((PEERS,), jnp.int32),
            pltpu.SMEM((PEERS,), jnp.int32),
            dma((ROUNDS, PEERS)),
            dma((ROUNDS, PEERS)),
            dma((ROUNDS, Z + 1)),
            dma((ROUNDS, Z, 3)),
            dma((ROUNDS, 3)),
            dma((ROUNDS, PEERS + X)),
            dma((4,)),
            dma((3,)),
            dma((ROUNDS, HEADS)),
            dma((ROUNDS, HEADS)),
            dma((ROUNDS, TILES, 6)),
            dma((ROUNDS, TILES, 2)),
            dma((ROUNDS, TILES, 2, 2)),
            dma((ROUNDS, HEADS, 2)),
            dma((ROUNDS, TILES)),
        ],
        compiler_params=pltpu.CompilerParams(
            collective_id=0, has_side_effects=True, vmem_limit_bytes=60 * 1024 * 1024
        ),
        cost_estimate=pl.CostEstimate(
            flops=72 * 4 * BLOCK * BLOCK * HEAD,
            bytes_accessed=8 * 1024 * 1024,
            transcendentals=72 * BLOCK * BLOCK,
        ),
        name="attend_and_project",
    )(selected.transpose(0, 3, 1, 2), length, queries, keys, values, out_weight)
    attended = attended.reshape(ROUNDS, BLOCK, HEADS * HEAD)
    return pl.pallas_call(
        hand_over,
        out_shape=(
            jax.ShapeDtypeStruct(attended.shape, bf16),
            jax.ShapeDtypeStruct(projected.shape, bf16),
        ),
        in_specs=[anywhere, anywhere],
        out_specs=(anywhere, anywhere),
        scratch_shapes=[dma((8,))],
        name="hand_over",
    )(attended, projected)


def solution(mesh):
    placed = (
        P(None, "seq", "head"),
        P(None, "seq", "head"),
        P(None, "seq", "head"),
        P(None, "seq", "head", None),
        P(),
        P("head", None),
    )
    return jax.shard_map(
        per_device,
        mesh=mesh,
        in_specs=placed,
        out_specs=(P(None, "seq", "head"), P(None, ("seq", "head"), None)),
        check_vma=False,
    )
```

```python
import jax
import jax.numpy as jnp
from jax import lax
from jax.experimental import pallas as pl
from jax.experimental.pallas import tpu as pltpu
from jax.sharding import PartitionSpec as P

HEAD = 128
Z, X, Y = 8, 4, 4
PEERS = Z * X
BLOCK = 512
HEADS = 4
TOPK = 3
ROUNDS = 2
MODEL = 4096
GAIN = HEAD ** (-0.5) * 1.4426950408889634
CUT = 304
COLS = 1024
HALF = COLS // 2
TILES = MODEL // COLS
MESH = pl.DeviceIdType.MESH
STEPS = 104
FORWARD = (
    4989827, 8718083, 0, 9381394, 8914067, 49, 42729747, 26531,
    3294785, 91661, 114066482, 17720832, 103546905, 36438016, 118248259, 99867,
    70202880, 79386, 57, 74405419, 87562, 15488073, 15431168, 0,
    78418944, 19895995, 53376512, 169472, 0, 0, 0, 0,
    0, 0, 0,
)
WORK = (
    0, 6815744, 15229962, 0, 8650752, 105129345, 17425, 42206208,
    33816625, 67584512, 71565601, 17039505, 11231745, 103178929, 9, 84247489,
    17923, 6563379, 5245337, 9437184, 73689088, 5722624, 10834569, 115634953,
    40110645, 119799993, 52843081, 3052345, 7099963, 7346213, 7632940, 3435565,
    9972742, 12074045, 31758,
)


def soft_part(key_tile, value_t, query_t, mask_from=None):
    scores = jnp.dot(key_tile, query_t, preferred_element_type=jnp.float32)
    if mask_from is not None:
        key_at = lax.broadcasted_iota(jnp.int32, scores.shape, 0)
        query_at = lax.broadcasted_iota(jnp.int32, scores.shape, 1) + mask_from
        scores = jnp.where(key_at <= query_at, scores, -1e30)
    highest = jnp.max(scores, axis=0, keepdims=True)
    weights = jnp.exp2((scores - highest) * GAIN)
    total = jnp.sum(weights, axis=0, keepdims=True)
    mixed = jnp.dot(value_t, weights.astype(jnp.bfloat16), preferred_element_type=jnp.float32)
    return mixed, highest, total


def value_rows(stacked):
    return jnp.concatenate([stacked[c * HEAD : (c + 1) * HEAD] for c in range(4)], axis=1)


def kernel(
    sel_ref, len_ref, q_ref, k_ref, v_ref, w_ref,
    att_ref, out_ref,
    kv, qv, vv, qt, us, ms, ls, wo, ws, attx, sib, part, relay, fin, outv, tile_of, round_of,
    ra, rb, saz, sax, sbx, sbz, insem, wsem, att_s, att_r, rs_s, relay_r, fin_r, att_o, out_o,
):
    seq = lax.axis_index("seq")
    head = lax.axis_index("head")
    z, x = seq // X, lax.rem(seq, X)
    y, core = head // 2, lax.rem(head, 2)

    def at(zz, xx):
        return lax.rem(zz + 2 * Z, Z) * X + lax.rem(xx + 2 * X, X)

    up, down = at(z + 1, x), at(z - 1, x)
    right, left = at(z, x + 1), at(z, x - 1)
    front = lax.rem(y + 1, Y) * 2 + core
    back = lax.rem(y + 3, Y) * 2 + core
    twin = y * 2 + 1 - core

    barrier = pltpu.get_barrier_semaphore()
    for peer in (up, down, right, left):
        pl.semaphore_signal(barrier, inc=1, device_id={"seq": peer}, device_id_type=MESH)
    for peer in (front, back, twin):
        pl.semaphore_signal(barrier, inc=1, device_id={"head": peer}, device_id_type=MESH)

    load_v = pltpu.make_async_copy(v_ref, vv, insem.at[0])
    load_k = [
        pltpu.make_async_copy(k_ref.at[r], kv.at[r, seq, 0], insem.at[1 + r]) for r in range(ROUNDS)
    ]
    load_q = pltpu.make_async_copy(q_ref, qv, insem.at[3])
    load_w = pltpu.make_async_copy(w_ref, wo, wsem.at[2])
    load_v.start()
    for load in load_k:
        load.start()
    load_q.start()
    load_v.wait()
    for r in range(ROUNDS):
        for c in range(4):
            rows = slice(c * HEAD, (c + 1) * HEAD)
            kv[r, seq, 1, rows, :] = vv[r, rows, :].T
    for load in load_k:
        load.wait()
    pl.semaphore_wait(barrier, 7)

    def copy_a(r, block, peer, send):
        view = kv.at[r, block, :, pl.ds(0, CUT), :]
        return pltpu.make_async_remote_copy(
            src_ref=view, dst_ref=view, send_sem=send, recv_sem=ra.at[r, block],
            device_id={"seq": peer}, device_id_type=MESH,
        )

    def copy_b(r, block, peer, send):
        view = kv.at[r, block, :, pl.ds(CUT, BLOCK - CUT), :]
        return pltpu.make_async_remote_copy(
            src_ref=view, dst_ref=view, send_sem=send, recv_sem=rb.at[r, block],
            device_id={"seq": peer}, device_id_type=MESH,
        )

    def wait_a(r, block):
        copy_a(r, block, up, saz.at[r, 8]).wait_recv()

    def wait_b(r, block):
        copy_b(r, block, up, sbz.at[r, 32]).wait_recv()

    def launch_b(r, act):
        act(copy_b(r, seq, right, sbx.at[r, 0]))
        act(copy_b(r, seq, left, sbx.at[r, 1]))
        act(copy_b(r, seq, up, sbz.at[r, seq]))
        act(copy_b(r, seq, down, sbz.at[r, 32 + x]))

    def launch_a(r, act):
        act(copy_a(r, seq, up, saz.at[r, z]))
        act(copy_a(r, seq, down, saz.at[r, 8]))
        act(copy_a(r, seq, right, sax.at[r, z, 0]))
        act(copy_a(r, seq, left, sax.at[r, z, 1]))

    def inner_of(k):
        return jnp.logical_and(k > 0, k < Z // 2)

    def below(r, k):
        return jnp.logical_or(
            jnp.logical_and(k == 0, r == 0), jnp.logical_and(k == Z // 2, r == 1)
        )

    def forward_a(r, k, act, waits):
        lo_z, hi_z = lax.rem(z + Z - k, Z), lax.rem(z + k, Z)
        lo, hi = at(lo_z, x), at(hi_z, x)
        if waits:
            wait_a(r, lo)

        @pl.when(jnp.logical_or(k < 3, jnp.logical_and(k == 3, r == 0)))
        def _():
            act(copy_a(r, lo, up, saz.at[r, lo_z]))

        act(copy_a(r, lo, right, sax.at[r, lo_z, 0]))
        act(copy_a(r, lo, left, sax.at[r, lo_z, 1]))

        @pl.when(k < 4)
        def _():
            if waits:
                wait_a(r, hi)

            @pl.when(jnp.logical_or(k < 3, r == 1))
            def _():
                act(copy_a(r, hi, down, saz.at[r, hi_z]))

            act(copy_a(r, hi, right, sax.at[r, hi_z, 0]))
            act(copy_a(r, hi, left, sax.at[r, hi_z, 1]))

    def forward_f(r, k, act, waits):
        lo_z, hi_z = lax.rem(z + Z - k, Z), lax.rem(z + k, Z)
        inner, is_below = inner_of(k), below(r, k)

        @pl.when(jnp.logical_or(inner, is_below))
        def _():
            block = at(lo_z, x - 1)
            if waits:
                wait_a(r, block)
            act(copy_a(r, block, right, sax.at[r, lo_z, 2]))

        @pl.when(jnp.logical_or(inner, jnp.logical_not(is_below)))
        def _():
            block = at(hi_z, x + 1)
            if waits:
                wait_a(r, block)
            act(copy_a(r, block, left, sax.at[r, hi_z, 2]))

    def forward_b(r, k, off, act, waits):
        lo_z, hi_z = lax.rem(z + Z - k, Z), lax.rem(z + k, Z)
        col = lax.rem(x + off, X)
        lo, hi = at(lo_z, col), at(hi_z, col)
        if waits:
            wait_b(r, lo)

        @pl.when(k == 0)
        def _():
            @pl.when(jnp.logical_and(off == 1, r == 1))
            def _():
                act(copy_b(r, lo, left, sbx.at[r, 2]))

            @pl.when(jnp.logical_and(off == 3, r == 0))
            def _():
                act(copy_b(r, lo, right, sbx.at[r, 2]))

            act(copy_b(r, lo, up, sbz.at[r, lo]))
            act(copy_b(r, lo, down, sbz.at[r, 32 + col]))

        @pl.when(k > 0)
        def _():
            @pl.when(jnp.logical_or(k < 3, jnp.logical_and(k == 3, lax.rem(col, 2) == 0)))
            def _():
                act(copy_b(r, lo, up, sbz.at[r, lo]))

            @pl.when(k < 4)
            def _():
                if waits:
                    wait_b(r, hi)

                @pl.when(jnp.logical_or(k < 3, lax.rem(col, 2) == 1))
                def _():
                    act(copy_b(r, hi, down, sbz.at[r, hi]))

    def far_tile(r, block):
        query_t = qt.at[tile_of[block]]
        newer = round_of[block] == 1
        key_tile = jnp.where(newer, kv[r, block, 0], kv[0, block, 0])
        value_t = value_rows(jnp.where(newer, kv[r, block, 1], kv[0, block, 1]))
        for c in range(2):
            cols = slice(c * 256, (c + 1) * 256)
            mixed, highest, total = soft_part(key_tile, value_t, query_t[:, cols])
            us[block, :, cols] = mixed
            ms[block, :, cols] = highest
            ls[block, :, cols] = total

    def own_tile(r, h):
        tile = r * HEADS + h
        key_tile = kv[r, seq, 0]
        value_t = value_rows(kv[r, seq, 1])
        for c in range(2):
            cols = slice(c * 256, (c + 1) * 256)
            keys_to = (c + 1) * 256
            mixed, highest, total = soft_part(
                key_tile[:keys_to], value_t[:, :keys_to], qt[tile, :, cols], c * 256
            )
            us[PEERS + tile, :, cols] = mixed
            ms[PEERS + tile, :, cols] = highest
            ls[PEERS + tile, :, cols] = total

    def far_slots(r, k, off):
        inner, is_below = inner_of(k), below(r, k)

        def one(side, carry):
            zz = jnp.where(side == 0, z + Z - k, z + k)
            block = at(zz, x + off)
            from_left = jnp.where(inner, side == 0, is_below)
            live = jnp.logical_or(side == 0, inner)
            pending = jnp.logical_or(
                off == 2,
                jnp.logical_or(
                    jnp.logical_and(from_left, off == 1),
                    jnp.logical_and(jnp.logical_not(from_left), off == 3),
                ),
            )

            @pl.when(jnp.logical_and(live, pending))
            def _():
                wait_a(r, block)

            @pl.when(jnp.logical_and(live, jnp.logical_or(r == 0, block < seq)))
            def _():
                far_tile(r, block)

            return carry

        lax.fori_loop(0, 2, one, 0)

    def copy_att(r, h):
        return pltpu.make_async_remote_copy(
            src_ref=attx.at[r, 1 - core, h], dst_ref=sib.at[r, h],
            send_sem=att_s.at[r, h], recv_sem=att_r.at[r, h],
            device_id={"head": twin}, device_id_type=MESH,
        )

    def store_att(r, h, c):
        cols = pl.ds(pl.multiple_of(h * HEAD, HEAD), HEAD)
        return pltpu.make_async_copy(
            attx.at[r, c, h], att_ref.at[r, :, c, :, cols], att_o.at[r, h, c]
        )

    def merge(r, h):
        tile = r * HEADS + h
        own = PEERS + tile
        slots, oks = [], []
        top = ms[own]
        for j in range(TOPK):
            chosen = sel_ref[r, j, 0, h]
            ok = chosen < r * PEERS + seq
            slot = jnp.where(ok, lax.rem(chosen, PEERS), 0)
            slots.append(slot)
            oks.append(ok)
            top = jnp.maximum(top, jnp.where(ok, ms[slot], top))
        weights = [jnp.exp2((ms[own] - top) * GAIN)]
        whole = weights[0] * ls[own]
        for slot, ok in zip(slots, oks):
            weight = jnp.where(ok, jnp.exp2(jnp.minimum(ms[slot] - top, 0.0) * GAIN), 0.0)
            weights.append(weight)
            whole = whole + weight * ls[slot]
        row = lax.broadcasted_iota(jnp.int32, (1, BLOCK), 1)
        alive = row < len_ref[0] - (r * PEERS + seq) * BLOCK
        norm = jnp.where(alive, 1.0 / whole, 0.0)
        mixed = us[own] * (weights[0] * norm)
        for slot, weight in zip(slots, weights[1:]):
            mixed = mixed + us[slot] * (weight * norm)
        rows = mixed.T.astype(jnp.bfloat16).reshape(Y, 2, 64, HEAD)
        for c in range(2):
            attx[r, c, h] = rows[:, c]
        copy_att(r, h).start()
        for c in range(2):
            store_att(r, h, c).start()

    def copy_w():
        return pltpu.make_async_remote_copy(
            src_ref=w_ref, dst_ref=ws, send_sem=wsem.at[0], recv_sem=wsem.at[1],
            device_id={"head": twin}, device_id_type=MESH,
        )

    y_across, y_front, y_back = lax.rem(y + 2, Y), lax.rem(y + 1, Y), lax.rem(y + 3, Y)

    def copy_relay(r, n, side):
        return pltpu.make_async_remote_copy(
            src_ref=part.at[r, n, y_across, side], dst_ref=relay.at[r, n, side],
            send_sem=rs_s.at[r, n, side], recv_sem=relay_r.at[r, n, side],
            device_id={"head": front if side == 0 else back}, device_id_type=MESH,
        )

    def copy_fin(r, n, side, half):
        return pltpu.make_async_remote_copy(
            src_ref=part.at[r, n, y_front if side == 0 else y_back, half],
            dst_ref=fin.at[r, n, side, half],
            send_sem=rs_s.at[r, n, 2 + side * 2 + half], recv_sem=fin_r.at[r, n, side, half],
            device_id={"head": front if side == 0 else back}, device_id_type=MESH,
        )

    def project(r, n):
        own_rows = jnp.concatenate(
            [attx[r, core, h].reshape(Y * 64, HEAD) for h in range(HEADS)], axis=1
        )
        twin_rows = jnp.concatenate(
            [sib[r, h].reshape(Y * 64, HEAD) for h in range(HEADS)], axis=1
        )
        for half in range(2):
            cols = pl.ds(pl.multiple_of(n * COLS + half * HALF, HALF), HALF)
            term = jnp.dot(own_rows, wo[:, cols], preferred_element_type=jnp.float32)
            term = term + jnp.dot(twin_rows, ws[:, cols], preferred_element_type=jnp.float32)
            part[r, n, :, half] = term.astype(jnp.bfloat16).reshape(Y, 64, HALF)
        copy_relay(r, n, 0).start()
        copy_relay(r, n, 1).start()
        copy_fin(r, n, 0, 1).start()
        copy_fin(r, n, 1, 0).start()

    def pass_on(r, n):
        for side, target, half in ((0, y_front, 0), (1, y_back, 1)):
            copy_relay(r, n, side).wait_recv()
            total = part[r, n, target, half].astype(jnp.float32)
            total = total + relay[r, n, side].astype(jnp.float32)
            part[r, n, target, half] = total.astype(jnp.bfloat16)
            copy_fin(r, n, side, half).start()

    def store_out(r, n):
        cols = pl.ds(pl.multiple_of(n * COLS, COLS), COLS)
        return pltpu.make_async_copy(outv.at[r, :, cols], out_ref.at[r, :, cols], out_o.at[r, n])

    def finish(r, n):
        for side in range(2):
            for half in range(2):
                copy_fin(r, n, side, half).wait_recv()
        for half in range(2):
            total = part[r, n, y, half].astype(jnp.float32)
            total = total + fin[r, n, 0, half].astype(jnp.float32)
            total = total + fin[r, n, 1, half].astype(jnp.float32)
            cols = pl.ds(pl.multiple_of(n * COLS + half * HALF, HALF), HALF)
            outv[r, :, cols] = total.astype(jnp.bfloat16)
        store_out(r, n).start()

    start = lambda copy: copy.start()
    drain = lambda copy: copy.wait_send()

    launch_b(0, start)
    launch_a(0, start)
    copy_w().start()
    load_w.start()

    def table(block, carry):
        tile, newer = jnp.int32(0), jnp.int32(0)
        for r in range(ROUNDS):
            for h in range(HEADS):
                for j in range(TOPK):
                    chosen = sel_ref[r, j, 0, h]
                    hit = jnp.logical_and(
                        lax.rem(chosen, PEERS) == block, chosen < r * PEERS + seq
                    )
                    tile = jnp.where(hit, r * HEADS + h, tile)
                    newer = jnp.where(hit, chosen // PEERS, newer)
        tile_of[block] = tile
        round_of[block] = newer
        return carry

    load_q.wait()
    for r in range(ROUNDS):
        for h in range(HEADS):
            qt[r * HEADS + h] = qv[r, :, h * HEAD : (h + 1) * HEAD].T
    lax.fori_loop(0, PEERS, table, 0)

    def step(t, carry):
        forward, work_code = jnp.int32(FORWARD[0]), jnp.int32(WORK[0])
        third = t // 3
        for w in range(1, len(FORWARD)):
            here = third == w
            forward = jnp.where(here, FORWARD[w], forward)
            work_code = jnp.where(here, WORK[w], work_code)
        bits = lax.rem(t, 3) * 9
        forward, work_code = forward >> bits, work_code >> bits
        kind, r, k, off = forward & 7, (forward >> 3) & 1, (forward >> 4) & 7, (forward >> 7) & 3

        @pl.when(kind == 1)
        def _():
            forward_a(r, k, start, True)

        @pl.when(kind == 2)
        def _():
            forward_f(r, k, start, True)

        @pl.when(kind == 3)
        def _():
            forward_b(r, k, off, start, True)

        @pl.when(kind == 4)
        def _():
            launch_a(1, start)

        @pl.when(kind == 5)
        def _():
            launch_b(1, start)

        work, wr = work_code & 7, (work_code >> 3) & 1
        item, woff = (work_code >> 4) & 7, (work_code >> 7) & 3

        @pl.when(work == 1)
        def _():
            far_slots(wr, item, woff)

        @pl.when(work == 2)
        def _():
            own_tile(wr, item)

        @pl.when(work == 3)
        def _():
            merge(wr, item)

        @pl.when(work == 4)
        def _():
            @pl.when(item == 0)
            def _():
                @pl.when(wr == 0)
                def _():
                    load_w.wait()
                    copy_w().wait_recv()

                for h in range(HEADS):
                    copy_att(wr, h).wait_recv()

            project(wr, item)

        @pl.when(work == 5)
        def _():
            pass_on(wr, item)

        @pl.when(work == 6)
        def _():
            finish(wr, item)

        return carry

    lax.fori_loop(0, STEPS, step, 0)

    def drain_step(t, carry):
        r, k, off = t // 20, lax.rem(t // 4, 5), lax.rem(t, 4)

        @pl.when(jnp.logical_or(k > 0, off > 0))
        def _():
            forward_b(r, k, off, drain, False)

        @pl.when(off == 0)
        def _():
            forward_f(r, k, drain, False)

        @pl.when(jnp.logical_and(off == 0, k > 0))
        def _():
            forward_a(r, k, drain, False)

        return carry

    for r in range(ROUNDS):
        launch_a(r, drain)
        launch_b(r, drain)
    lax.fori_loop(0, ROUNDS * 20, drain_step, 0)
    copy_w().wait_send()

    def drain_sum(t, carry):
        r, n = t // TILES, lax.rem(t, TILES)
        copy_att(r, n).wait_send()
        for c in range(2):
            store_att(r, n, c).wait()
        for side in range(2):
            copy_relay(r, n, side).wait_send()
            for half in range(2):
                copy_fin(r, n, side, half).wait_send()
        store_out(r, n).wait()
        return carry

    lax.fori_loop(0, ROUNDS * TILES, drain_sum, 0)


def hand_over(att_in, out_in, att_ref, out_ref, att_v, out_v, sems):
    places = []
    for r in range(ROUNDS):
        for i in range(2):
            rows = slice(i * 256, (i + 1) * 256)
            places.append((att_in, att_v, att_ref, r, rows))
            rows = slice(i * 32, (i + 1) * 32)
            places.append((out_in, out_v, out_ref, r, rows))
    loads, stores = [], []
    for i, (src, mid, dst, r, rows) in enumerate(places):
        loads.append(
            pltpu.make_async_copy(src.at[r, rows, :], mid.at[r, rows, :], sems.at[0, i])
        )
        stores.append(
            pltpu.make_async_copy(mid.at[r, rows, :], dst.at[r, rows, :], sems.at[1, i])
        )
    for load in loads:
        load.start()
    for load, store in zip(loads, stores):
        load.wait()
        store.start()
    for store in stores:
        store.wait()


def per_device(queries, keys, values, selected, length, out_weight):
    anywhere = pl.BlockSpec(memory_space=pl.ANY)
    smem = pl.BlockSpec(memory_space=pltpu.SMEM)
    bf16, f32 = jnp.bfloat16, jnp.float32
    dma = pltpu.SemaphoreType.DMA
    attended, projected = pl.pallas_call(
        kernel,
        out_shape=(
            jax.ShapeDtypeStruct((ROUNDS, Y, 2, 64, HEADS * HEAD), bf16),
            jax.ShapeDtypeStruct((ROUNDS, 64, MODEL), bf16),
        ),
        in_specs=[smem, smem, anywhere, anywhere, anywhere, anywhere],
        out_specs=(anywhere, anywhere),
        scratch_shapes=[
            pltpu.VMEM((ROUNDS, PEERS, 2, BLOCK, HEAD), bf16),
            pltpu.VMEM((ROUNDS, BLOCK, HEADS * HEAD), bf16),
            pltpu.VMEM((ROUNDS, BLOCK, HEAD), bf16),
            pltpu.VMEM((ROUNDS * HEADS, HEAD, BLOCK), bf16),
            pltpu.VMEM((PEERS + ROUNDS * HEADS, HEAD, BLOCK), f32),
            pltpu.VMEM((PEERS + ROUNDS * HEADS, 1, BLOCK), f32),
            pltpu.VMEM((PEERS + ROUNDS * HEADS, 1, BLOCK), f32),
            pltpu.VMEM((HEADS * HEAD, MODEL), bf16),
            pltpu.VMEM((HEADS * HEAD, MODEL), bf16),
            pltpu.VMEM((ROUNDS, 2, HEADS, Y, 64, HEAD), bf16),
            pltpu.VMEM((ROUNDS, HEADS, Y, 64, HEAD), bf16),
            pltpu.VMEM((ROUNDS, TILES, Y, 2, 64, HALF), bf16),
            pltpu.VMEM((ROUNDS, TILES, 2, 64, HALF), bf16),
            pltpu.VMEM((ROUNDS, TILES, 2, 2, 64, HALF), bf16),
            pltpu.VMEM((ROUNDS, 64, MODEL), bf16),
            pltpu.SMEM((PEERS,), jnp.int32),
            pltpu.SMEM((PEERS,), jnp.int32),
            dma((ROUNDS, PEERS)),
            dma((ROUNDS, PEERS)),
            dma((ROUNDS, Z + 1)),
            dma((ROUNDS, Z, 3)),
            dma((ROUNDS, 3)),
            dma((ROUNDS, PEERS + X)),
            dma((4,)),
            dma((3,)),
            dma((ROUNDS, HEADS)),
            dma((ROUNDS, HEADS)),
            dma((ROUNDS, TILES, 6)),
            dma((ROUNDS, TILES, 2)),
            dma((ROUNDS, TILES, 2, 2)),
            dma((ROUNDS, HEADS, 2)),
            dma((ROUNDS, TILES)),
        ],
        compiler_params=pltpu.CompilerParams(
            collective_id=0, has_side_effects=True, vmem_limit_bytes=60 * 1024 * 1024
        ),
        cost_estimate=pl.CostEstimate(
            flops=72 * 4 * BLOCK * BLOCK * HEAD,
            bytes_accessed=8 * 1024 * 1024,
            transcendentals=72 * BLOCK * BLOCK,
        ),
        name="attend_and_project",
    )(selected.transpose(0, 3, 1, 2), length, queries, keys, values, out_weight)
    attended = attended.reshape(ROUNDS, BLOCK, HEADS * HEAD)
    return pl.pallas_call(
        hand_over,
        out_shape=(
            jax.ShapeDtypeStruct(attended.shape, bf16),
            jax.ShapeDtypeStruct(projected.shape, bf16),
        ),
        in_specs=[anywhere, anywhere],
        out_specs=(anywhere, anywhere),
        scratch_shapes=[
            pltpu.VMEM(attended.shape, bf16),
            pltpu.VMEM(projected.shape, bf16),
            dma((2, 8)),
        ],
        compiler_params=pltpu.CompilerParams(vmem_limit_bytes=60 * 1024 * 1024),
        name="hand_over",
    )(attended, projected)


def solution(mesh):
    placed = (
        P(None, "seq", "head"),
        P(None, "seq", "head"),
        P(None, "seq", "head"),
        P(None, "seq", "head", None),
        P(),
        P("head", None),
    )
    return jax.shard_map(
        per_device,
        mesh=mesh,
        in_specs=placed,
        out_specs=(P(None, "seq", "head"), P(None, ("seq", "head"), None)),
        check_vma=False,
    )
```

```python
import jax
import jax.numpy as jnp
from jax import lax
from jax.experimental import pallas as pl
from jax.experimental.pallas import tpu as pltpu
from jax.sharding import PartitionSpec as P

HEAD = 128
Z, X, Y = 8, 4, 4
PEERS = Z * X
BLOCK = 512
HEADS = 4
TOPK = 3
ROUNDS = 2
MODEL = 4096
GAIN = HEAD ** (-0.5) * 1.4426950408889634
CUT = 304
COLS = 1024
HALF = COLS // 2
TILES = MODEL // COLS
MESH = pl.DeviceIdType.MESH
STEPS = 104
FORWARD = (
    4989827, 8718083, 0, 9381394, 8914067, 49, 42729747, 26531,
    3294785, 91661, 114066482, 17720832, 103546905, 36438016, 118248259, 99867,
    70202880, 79386, 57, 74405419, 87562, 15488073, 15431168, 0,
    78418944, 19895995, 53376512, 169472, 0, 0, 0, 0,
    0, 0, 0,
)
WORK = (
    0, 6815744, 15229962, 0, 8650752, 105129345, 17425, 42206208,
    33816625, 67584512, 71565601, 17039505, 11231745, 103178929, 9, 84247489,
    17923, 6563379, 5245337, 9437184, 73689088, 5722624, 10834569, 115634953,
    40110645, 119799993, 52843081, 3052345, 7099963, 7346213, 7632940, 3435565,
    9972742, 12074045, 31758,
)


def soft_part(key_tile, value_t, query_t, mask_from=None):
    scores = jnp.dot(key_tile, query_t, preferred_element_type=jnp.float32)
    if mask_from is not None:
        key_at = lax.broadcasted_iota(jnp.int32, scores.shape, 0)
        query_at = lax.broadcasted_iota(jnp.int32, scores.shape, 1) + mask_from
        scores = jnp.where(key_at <= query_at, scores, -1e30)
    highest = jnp.max(scores, axis=0, keepdims=True)
    weights = jnp.exp2((scores - highest) * GAIN)
    total = jnp.sum(weights, axis=0, keepdims=True)
    mixed = jnp.dot(value_t, weights.astype(jnp.bfloat16), preferred_element_type=jnp.float32)
    return mixed, highest, total


def value_rows(stacked):
    return jnp.concatenate([stacked[c * HEAD : (c + 1) * HEAD] for c in range(4)], axis=1)


def kernel(
    sel_ref, len_ref, q_ref, k_ref, v_ref, w_ref,
    att_ref, out_ref,
    kv, qv, vv, qt, us, ms, ls, wo, ws, attx, sib, part, relay, fin, outv, tile_of, round_of,
    ra, rb, saz, sax, sbx, sbz, insem, wsem, att_s, att_r, rs_s, relay_r, fin_r, att_o, out_o,
):
    seq = lax.axis_index("seq")
    head = lax.axis_index("head")
    z, x = seq // X, lax.rem(seq, X)
    y, core = head // 2, lax.rem(head, 2)

    def at(zz, xx):
        return lax.rem(zz + 2 * Z, Z) * X + lax.rem(xx + 2 * X, X)

    up, down = at(z + 1, x), at(z - 1, x)
    right, left = at(z, x + 1), at(z, x - 1)
    front = lax.rem(y + 1, Y) * 2 + core
    back = lax.rem(y + 3, Y) * 2 + core
    twin = y * 2 + 1 - core

    barrier = pltpu.get_barrier_semaphore()
    for peer in (up, down, right, left):
        pl.semaphore_signal(barrier, inc=1, device_id={"seq": peer}, device_id_type=MESH)
    for peer in (front, back, twin):
        pl.semaphore_signal(barrier, inc=1, device_id={"head": peer}, device_id_type=MESH)

    load_v = pltpu.make_async_copy(v_ref, vv, insem.at[0])
    load_k = [
        pltpu.make_async_copy(k_ref.at[r], kv.at[r, seq, 0], insem.at[1 + r]) for r in range(ROUNDS)
    ]
    load_q = pltpu.make_async_copy(q_ref, qv, insem.at[3])
    load_w = pltpu.make_async_copy(w_ref, wo, wsem.at[2])
    load_v.start()
    for load in load_k:
        load.start()
    load_q.start()
    load_v.wait()
    for r in range(ROUNDS):
        for c in range(4):
            rows = slice(c * HEAD, (c + 1) * HEAD)
            kv[r, seq, 1, rows, :] = vv[r, rows, :].T
    for load in load_k:
        load.wait()
    pl.semaphore_wait(barrier, 7)

    def copy_a(r, block, peer, send):
        view = kv.at[r, block, :, pl.ds(0, CUT), :]
        return pltpu.make_async_remote_copy(
            src_ref=view, dst_ref=view, send_sem=send, recv_sem=ra.at[r, block],
            device_id={"seq": peer}, device_id_type=MESH,
        )

    def copy_b(r, block, peer, send):
        view = kv.at[r, block, :, pl.ds(CUT, BLOCK - CUT), :]
        return pltpu.make_async_remote_copy(
            src_ref=view, dst_ref=view, send_sem=send, recv_sem=rb.at[r, block],
            device_id={"seq": peer}, device_id_type=MESH,
        )

    def wait_a(r, block):
        copy_a(r, block, up, saz.at[r, 8]).wait_recv()

    def wait_b(r, block):
        copy_b(r, block, up, sbz.at[r, 32]).wait_recv()

    def launch_b(r, act):
        act(copy_b(r, seq, right, sbx.at[r, 0]))
        act(copy_b(r, seq, left, sbx.at[r, 1]))
        act(copy_b(r, seq, up, sbz.at[r, seq]))
        act(copy_b(r, seq, down, sbz.at[r, 32 + x]))

    def launch_a(r, act):
        act(copy_a(r, seq, up, saz.at[r, z]))
        act(copy_a(r, seq, down, saz.at[r, 8]))
        act(copy_a(r, seq, right, sax.at[r, z, 0]))
        act(copy_a(r, seq, left, sax.at[r, z, 1]))

    def inner_of(k):
        return jnp.logical_and(k > 0, k < Z // 2)

    def below(r, k):
        return jnp.logical_or(
            jnp.logical_and(k == 0, r == 0), jnp.logical_and(k == Z // 2, r == 1)
        )

    def forward_a(r, k, act, waits):
        lo_z, hi_z = lax.rem(z + Z - k, Z), lax.rem(z + k, Z)
        lo, hi = at(lo_z, x), at(hi_z, x)
        if waits:
            wait_a(r, lo)

        @pl.when(jnp.logical_or(k < 3, jnp.logical_and(k == 3, r == 0)))
        def _():
            act(copy_a(r, lo, up, saz.at[r, lo_z]))

        act(copy_a(r, lo, right, sax.at[r, lo_z, 0]))
        act(copy_a(r, lo, left, sax.at[r, lo_z, 1]))

        @pl.when(k < 4)
        def _():
            if waits:
                wait_a(r, hi)

            @pl.when(jnp.logical_or(k < 3, r == 1))
            def _():
                act(copy_a(r, hi, down, saz.at[r, hi_z]))

            act(copy_a(r, hi, right, sax.at[r, hi_z, 0]))
            act(copy_a(r, hi, left, sax.at[r, hi_z, 1]))

    def forward_f(r, k, act, waits):
        lo_z, hi_z = lax.rem(z + Z - k, Z), lax.rem(z + k, Z)
        inner, is_below = inner_of(k), below(r, k)

        @pl.when(jnp.logical_or(inner, is_below))
        def _():
            block = at(lo_z, x - 1)
            if waits:
                wait_a(r, block)
            act(copy_a(r, block, right, sax.at[r, lo_z, 2]))

        @pl.when(jnp.logical_or(inner, jnp.logical_not(is_below)))
        def _():
            block = at(hi_z, x + 1)
            if waits:
                wait_a(r, block)
            act(copy_a(r, block, left, sax.at[r, hi_z, 2]))

    def forward_b(r, k, off, act, waits):
        lo_z, hi_z = lax.rem(z + Z - k, Z), lax.rem(z + k, Z)
        col = lax.rem(x + off, X)
        lo, hi = at(lo_z, col), at(hi_z, col)
        if waits:
            wait_b(r, lo)

        @pl.when(k == 0)
        def _():
            @pl.when(jnp.logical_and(off == 1, r == 1))
            def _():
                act(copy_b(r, lo, left, sbx.at[r, 2]))

            @pl.when(jnp.logical_and(off == 3, r == 0))
            def _():
                act(copy_b(r, lo, right, sbx.at[r, 2]))

            act(copy_b(r, lo, up, sbz.at[r, lo]))
            act(copy_b(r, lo, down, sbz.at[r, 32 + col]))

        @pl.when(k > 0)
        def _():
            @pl.when(jnp.logical_or(k < 3, jnp.logical_and(k == 3, lax.rem(col, 2) == 0)))
            def _():
                act(copy_b(r, lo, up, sbz.at[r, lo]))

            @pl.when(k < 4)
            def _():
                if waits:
                    wait_b(r, hi)

                @pl.when(jnp.logical_or(k < 3, lax.rem(col, 2) == 1))
                def _():
                    act(copy_b(r, hi, down, sbz.at[r, hi]))

    def far_tiles(r, blocks):
        def scores_of(block, cols):
            newer = round_of[block] == 1
            key_tile = jnp.where(newer, kv[r, block, 0], kv[0, block, 0])
            query_t = qt[tile_of[block], :, cols]
            return jnp.dot(key_tile, query_t, preferred_element_type=jnp.float32)

        def mix(block, cols, scores):
            newer = round_of[block] == 1
            value_t = value_rows(jnp.where(newer, kv[r, block, 1], kv[0, block, 1]))
            highest = jnp.max(scores, axis=0, keepdims=True)
            weights = jnp.exp2((scores - highest) * GAIN)
            ms[block, :, cols] = highest
            ls[block, :, cols] = jnp.sum(weights, axis=0, keepdims=True)
            us[block, :, cols] = jnp.dot(
                value_t, weights.astype(jnp.bfloat16), preferred_element_type=jnp.float32
            )

        parts = [(block, slice(c * 256, (c + 1) * 256)) for block in blocks for c in range(2)]
        scores = scores_of(*parts[0])
        for i, part_now in enumerate(parts):
            ahead = scores_of(*parts[i + 1]) if i + 1 < len(parts) else None
            mix(*part_now, scores)
            scores = ahead

    def own_tile(r, h):
        tile = r * HEADS + h
        key_tile = kv[r, seq, 0]
        value_t = value_rows(kv[r, seq, 1])
        for c in range(2):
            cols = slice(c * 256, (c + 1) * 256)
            keys_to = (c + 1) * 256
            mixed, highest, total = soft_part(
                key_tile[:keys_to], value_t[:, :keys_to], qt[tile, :, cols], c * 256
            )
            us[PEERS + tile, :, cols] = mixed
            ms[PEERS + tile, :, cols] = highest
            ls[PEERS + tile, :, cols] = total

    def far_slots(r, k, off):
        inner, is_below = inner_of(k), below(r, k)

        def block_of(side):
            return at(jnp.where(side == 0, z + Z - k, z + k), x + off)

        def useful(side):
            live = jnp.logical_or(side == 0, inner)
            return jnp.logical_and(live, jnp.logical_or(r == 0, block_of(side) < seq))

        def arrive(side, carry):
            from_left = jnp.where(inner, side == 0, is_below)
            live = jnp.logical_or(side == 0, inner)
            pending = jnp.logical_or(
                off == 2,
                jnp.logical_or(
                    jnp.logical_and(from_left, off == 1),
                    jnp.logical_and(jnp.logical_not(from_left), off == 3),
                ),
            )

            @pl.when(jnp.logical_and(live, pending))
            def _():
                wait_a(r, block_of(side))

            return carry

        lax.fori_loop(0, 2, arrive, 0)
        both = jnp.logical_and(useful(0), useful(1))

        @pl.when(both)
        def _():
            far_tiles(r, (block_of(0), block_of(1)))

        @pl.when(jnp.logical_not(both))
        def _():
            def one(side, carry):
                @pl.when(useful(side))
                def _():
                    far_tiles(r, (block_of(side),))

                return carry

            lax.fori_loop(0, 2, one, 0)

    def copy_att(r, h):
        return pltpu.make_async_remote_copy(
            src_ref=attx.at[r, 1 - core, h], dst_ref=sib.at[r, h],
            send_sem=att_s.at[r, h], recv_sem=att_r.at[r, h],
            device_id={"head": twin}, device_id_type=MESH,
        )

    def store_att(r, h, c):
        cols = pl.ds(pl.multiple_of(h * HEAD, HEAD), HEAD)
        return pltpu.make_async_copy(
            attx.at[r, c, h], att_ref.at[r, :, c, :, cols], att_o.at[r, h, c]
        )

    def merge(r, h):
        tile = r * HEADS + h
        own = PEERS + tile
        slots, oks = [], []
        top = ms[own]
        for j in range(TOPK):
            chosen = sel_ref[r, j, 0, h]
            ok = chosen < r * PEERS + seq
            slot = jnp.where(ok, lax.rem(chosen, PEERS), 0)
            slots.append(slot)
            oks.append(ok)
            top = jnp.maximum(top, jnp.where(ok, ms[slot], top))
        weights = [jnp.exp2((ms[own] - top) * GAIN)]
        whole = weights[0] * ls[own]
        for slot, ok in zip(slots, oks):
            weight = jnp.where(ok, jnp.exp2(jnp.minimum(ms[slot] - top, 0.0) * GAIN), 0.0)
            weights.append(weight)
            whole = whole + weight * ls[slot]
        row = lax.broadcasted_iota(jnp.int32, (1, BLOCK), 1)
        alive = row < len_ref[0] - (r * PEERS + seq) * BLOCK
        norm = jnp.where(alive, 1.0 / whole, 0.0)
        mixed = us[own] * (weights[0] * norm)
        for slot, weight in zip(slots, weights[1:]):
            mixed = mixed + us[slot] * (weight * norm)
        rows = mixed.T.astype(jnp.bfloat16).reshape(Y, 2, 64, HEAD)
        for c in range(2):
            attx[r, c, h] = rows[:, c]
        copy_att(r, h).start()
        for c in range(2):
            store_att(r, h, c).start()

    def copy_w():
        return pltpu.make_async_remote_copy(
            src_ref=w_ref, dst_ref=ws, send_sem=wsem.at[0], recv_sem=wsem.at[1],
            device_id={"head": twin}, device_id_type=MESH,
        )

    y_across, y_front, y_back = lax.rem(y + 2, Y), lax.rem(y + 1, Y), lax.rem(y + 3, Y)

    def copy_relay(r, n, side):
        return pltpu.make_async_remote_copy(
            src_ref=part.at[r, n, y_across, side], dst_ref=relay.at[r, n, side],
            send_sem=rs_s.at[r, n, side], recv_sem=relay_r.at[r, n, side],
            device_id={"head": front if side == 0 else back}, device_id_type=MESH,
        )

    def copy_fin(r, n, side, half):
        return pltpu.make_async_remote_copy(
            src_ref=part.at[r, n, y_front if side == 0 else y_back, half],
            dst_ref=fin.at[r, n, side, half],
            send_sem=rs_s.at[r, n, 2 + side * 2 + half], recv_sem=fin_r.at[r, n, side, half],
            device_id={"head": front if side == 0 else back}, device_id_type=MESH,
        )

    def project(r, n):
        own_rows = jnp.concatenate(
            [attx[r, core, h].reshape(Y * 64, HEAD) for h in range(HEADS)], axis=1
        )
        twin_rows = jnp.concatenate(
            [sib[r, h].reshape(Y * 64, HEAD) for h in range(HEADS)], axis=1
        )
        for half in range(2):
            cols = pl.ds(pl.multiple_of(n * COLS + half * HALF, HALF), HALF)
            term = jnp.dot(own_rows, wo[:, cols], preferred_element_type=jnp.float32)
            term = term + jnp.dot(twin_rows, ws[:, cols], preferred_element_type=jnp.float32)
            part[r, n, :, half] = term.astype(jnp.bfloat16).reshape(Y, 64, HALF)
        copy_relay(r, n, 0).start()
        copy_relay(r, n, 1).start()
        copy_fin(r, n, 0, 1).start()
        copy_fin(r, n, 1, 0).start()

    def pass_on(r, n):
        for side, target, half in ((0, y_front, 0), (1, y_back, 1)):
            copy_relay(r, n, side).wait_recv()
            total = part[r, n, target, half].astype(jnp.float32)
            total = total + relay[r, n, side].astype(jnp.float32)
            part[r, n, target, half] = total.astype(jnp.bfloat16)
            copy_fin(r, n, side, half).start()

    def store_out(r, n):
        cols = pl.ds(pl.multiple_of(n * COLS, COLS), COLS)
        return pltpu.make_async_copy(outv.at[r, :, cols], out_ref.at[r, :, cols], out_o.at[r, n])

    def finish(r, n):
        for side in range(2):
            for half in range(2):
                copy_fin(r, n, side, half).wait_recv()
        for half in range(2):
            total = part[r, n, y, half].astype(jnp.float32)
            total = total + fin[r, n, 0, half].astype(jnp.float32)
            total = total + fin[r, n, 1, half].astype(jnp.float32)
            cols = pl.ds(pl.multiple_of(n * COLS + half * HALF, HALF), HALF)
            outv[r, :, cols] = total.astype(jnp.bfloat16)
        store_out(r, n).start()

    start = lambda copy: copy.start()
    drain = lambda copy: copy.wait_send()

    launch_b(0, start)
    launch_a(0, start)
    copy_w().start()
    load_w.start()

    def table(block, carry):
        tile, newer = jnp.int32(0), jnp.int32(0)
        for r in range(ROUNDS):
            for h in range(HEADS):
                for j in range(TOPK):
                    chosen = sel_ref[r, j, 0, h]
                    hit = jnp.logical_and(
                        lax.rem(chosen, PEERS) == block, chosen < r * PEERS + seq
                    )
                    tile = jnp.where(hit, r * HEADS + h, tile)
                    newer = jnp.where(hit, chosen // PEERS, newer)
        tile_of[block] = tile
        round_of[block] = newer
        return carry

    load_q.wait()
    for r in range(ROUNDS):
        for h in range(HEADS):
            qt[r * HEADS + h] = qv[r, :, h * HEAD : (h + 1) * HEAD].T
    lax.fori_loop(0, PEERS, table, 0)

    def step(t, carry):
        forward, work_code = jnp.int32(FORWARD[0]), jnp.int32(WORK[0])
        third = t // 3
        for w in range(1, len(FORWARD)):
            here = third == w
            forward = jnp.where(here, FORWARD[w], forward)
            work_code = jnp.where(here, WORK[w], work_code)
        bits = lax.rem(t, 3) * 9
        forward, work_code = forward >> bits, work_code >> bits
        kind, r, k, off = forward & 7, (forward >> 3) & 1, (forward >> 4) & 7, (forward >> 7) & 3

        @pl.when(kind == 1)
        def _():
            forward_a(r, k, start, True)

        @pl.when(kind == 2)
        def _():
            forward_f(r, k, start, True)

        @pl.when(kind == 3)
        def _():
            forward_b(r, k, off, start, True)

        @pl.when(kind == 4)
        def _():
            launch_a(1, start)

        @pl.when(kind == 5)
        def _():
            launch_b(1, start)

        work, wr = work_code & 7, (work_code >> 3) & 1
        item, woff = (work_code >> 4) & 7, (work_code >> 7) & 3

        @pl.when(work == 1)
        def _():
            far_slots(wr, item, woff)

        @pl.when(work == 2)
        def _():
            own_tile(wr, item)

        @pl.when(work == 3)
        def _():
            merge(wr, item)

        @pl.when(work == 4)
        def _():
            @pl.when(item == 0)
            def _():
                @pl.when(wr == 0)
                def _():
                    load_w.wait()
                    copy_w().wait_recv()

                for h in range(HEADS):
                    copy_att(wr, h).wait_recv()

            project(wr, item)

        @pl.when(work == 5)
        def _():
            pass_on(wr, item)

        @pl.when(work == 6)
        def _():
            finish(wr, item)

        return carry

    lax.fori_loop(0, STEPS, step, 0)

    def drain_step(t, carry):
        r, k, off = t // 20, lax.rem(t // 4, 5), lax.rem(t, 4)

        @pl.when(jnp.logical_or(k > 0, off > 0))
        def _():
            forward_b(r, k, off, drain, False)

        @pl.when(off == 0)
        def _():
            forward_f(r, k, drain, False)

        @pl.when(jnp.logical_and(off == 0, k > 0))
        def _():
            forward_a(r, k, drain, False)

        return carry

    for r in range(ROUNDS):
        launch_a(r, drain)
        launch_b(r, drain)
    lax.fori_loop(0, ROUNDS * 20, drain_step, 0)
    copy_w().wait_send()

    def drain_sum(t, carry):
        r, n = t // TILES, lax.rem(t, TILES)
        copy_att(r, n).wait_send()
        for c in range(2):
            store_att(r, n, c).wait()
        for side in range(2):
            copy_relay(r, n, side).wait_send()
            for half in range(2):
                copy_fin(r, n, side, half).wait_send()
        store_out(r, n).wait()
        return carry

    lax.fori_loop(0, ROUNDS * TILES, drain_sum, 0)


def hand_over(att_in, out_in, att_ref, out_ref, att_v, out_v, sems):
    places = []
    for r in range(ROUNDS):
        for i in range(2):
            rows = slice(i * 256, (i + 1) * 256)
            places.append((att_in, att_v, att_ref, r, rows))
            rows = slice(i * 32, (i + 1) * 32)
            places.append((out_in, out_v, out_ref, r, rows))
    loads, stores = [], []
    for i, (src, mid, dst, r, rows) in enumerate(places):
        loads.append(
            pltpu.make_async_copy(src.at[r, rows, :], mid.at[r, rows, :], sems.at[0, i])
        )
        stores.append(
            pltpu.make_async_copy(mid.at[r, rows, :], dst.at[r, rows, :], sems.at[1, i])
        )
    for load in loads:
        load.start()
    for load, store in zip(loads, stores):
        load.wait()
        store.start()
    for store in stores:
        store.wait()


def per_device(queries, keys, values, selected, length, out_weight):
    anywhere = pl.BlockSpec(memory_space=pl.ANY)
    smem = pl.BlockSpec(memory_space=pltpu.SMEM)
    bf16, f32 = jnp.bfloat16, jnp.float32
    dma = pltpu.SemaphoreType.DMA
    attended, projected = pl.pallas_call(
        kernel,
        out_shape=(
            jax.ShapeDtypeStruct((ROUNDS, Y, 2, 64, HEADS * HEAD), bf16),
            jax.ShapeDtypeStruct((ROUNDS, 64, MODEL), bf16),
        ),
        in_specs=[smem, smem, anywhere, anywhere, anywhere, anywhere],
        out_specs=(anywhere, anywhere),
        scratch_shapes=[
            pltpu.VMEM((ROUNDS, PEERS, 2, BLOCK, HEAD), bf16),
            pltpu.VMEM((ROUNDS, BLOCK, HEADS * HEAD), bf16),
            pltpu.VMEM((ROUNDS, BLOCK, HEAD), bf16),
            pltpu.VMEM((ROUNDS * HEADS, HEAD, BLOCK), bf16),
            pltpu.VMEM((PEERS + ROUNDS * HEADS, HEAD, BLOCK), f32),
            pltpu.VMEM((PEERS + ROUNDS * HEADS, 1, BLOCK), f32),
            pltpu.VMEM((PEERS + ROUNDS * HEADS, 1, BLOCK), f32),
            pltpu.VMEM((HEADS * HEAD, MODEL), bf16),
            pltpu.VMEM((HEADS * HEAD, MODEL), bf16),
            pltpu.VMEM((ROUNDS, 2, HEADS, Y, 64, HEAD), bf16),
            pltpu.VMEM((ROUNDS, HEADS, Y, 64, HEAD), bf16),
            pltpu.VMEM((ROUNDS, TILES, Y, 2, 64, HALF), bf16),
            pltpu.VMEM((ROUNDS, TILES, 2, 64, HALF), bf16),
            pltpu.VMEM((ROUNDS, TILES, 2, 2, 64, HALF), bf16),
            pltpu.VMEM((ROUNDS, 64, MODEL), bf16),
            pltpu.SMEM((PEERS,), jnp.int32),
            pltpu.SMEM((PEERS,), jnp.int32),
            dma((ROUNDS, PEERS)),
            dma((ROUNDS, PEERS)),
            dma((ROUNDS, Z + 1)),
            dma((ROUNDS, Z, 3)),
            dma((ROUNDS, 3)),
            dma((ROUNDS, PEERS + X)),
            dma((4,)),
            dma((3,)),
            dma((ROUNDS, HEADS)),
            dma((ROUNDS, HEADS)),
            dma((ROUNDS, TILES, 6)),
            dma((ROUNDS, TILES, 2)),
            dma((ROUNDS, TILES, 2, 2)),
            dma((ROUNDS, HEADS, 2)),
            dma((ROUNDS, TILES)),
        ],
        compiler_params=pltpu.CompilerParams(
            collective_id=0, has_side_effects=True, vmem_limit_bytes=60 * 1024 * 1024
        ),
        cost_estimate=pl.CostEstimate(
            flops=72 * 4 * BLOCK * BLOCK * HEAD,
            bytes_accessed=8 * 1024 * 1024,
            transcendentals=72 * BLOCK * BLOCK,
        ),
        name="attend_and_project",
    )(selected.transpose(0, 3, 1, 2), length, queries, keys, values, out_weight)
    attended = attended.reshape(ROUNDS, BLOCK, HEADS * HEAD)
    return pl.pallas_call(
        hand_over,
        out_shape=(
            jax.ShapeDtypeStruct(attended.shape, bf16),
            jax.ShapeDtypeStruct(projected.shape, bf16),
        ),
        in_specs=[anywhere, anywhere],
        out_specs=(anywhere, anywhere),
        scratch_shapes=[
            pltpu.VMEM(attended.shape, bf16),
            pltpu.VMEM(projected.shape, bf16),
            dma((2, 8)),
        ],
        compiler_params=pltpu.CompilerParams(vmem_limit_bytes=60 * 1024 * 1024),
        name="hand_over",
    )(attended, projected)


def solution(mesh):
    placed = (
        P(None, "seq", "head"),
        P(None, "seq", "head"),
        P(None, "seq", "head"),
        P(None, "seq", "head", None),
        P(),
        P("head", None),
    )
    return jax.shard_map(
        per_device,
        mesh=mesh,
        in_specs=placed,
        out_specs=(P(None, "seq", "head"), P(None, ("seq", "head"), None)),
        check_vma=False,
    )
```

```python
import jax
import jax.numpy as jnp
from jax import lax
from jax.experimental import pallas as pl
from jax.experimental.pallas import tpu as pltpu
from jax.sharding import PartitionSpec as P

HEAD = 128
Z, X, Y = 8, 4, 4
PEERS = Z * X
BLOCK = 512
HEADS = 4
TOPK = 3
ROUNDS = 2
MODEL = 4096
GAIN = HEAD ** (-0.5) * 1.4426950408889634
CUT = 304
COLS = 1024
HALF = COLS // 2
TILES = MODEL // COLS
MESH = pl.DeviceIdType.MESH
STEPS = 104
FORWARD = (
    4457859, 5113475, 4793889, 206336, 72107008, 9200291, 3360547, 6721,
    114058240, 80504499, 36450816, 103777819, 51118146, 17729034, 10747904, 13579,
    155, 107741184, 11301376, 112080384, 11047595, 0, 153147, 58,
    116167680, 95744, 82575435, 104395, 331, 0, 0, 0,
    0, 0, 0,
)
WORK = (
    8912896, 0, 524314, 67379754, 15278593, 0, 100925449, 71771041,
    33833482, 4718592, 82609, 103022881, 25905, 35913728, 221761, 117727744,
    5079873, 922147, 5244979, 36, 44302388, 40127017, 111421952, 9974329,
    115605913, 48524057, 77894149, 82154441, 2905929, 3159611, 11562012, 3411004,
    3701277, 5782573, 23614,
)


def value_rows(stacked):
    return jnp.concatenate([stacked[c * HEAD : (c + 1) * HEAD] for c in range(4)], axis=1)


def kernel(
    sel_ref, len_ref, q_ref, k_ref, v_ref, w_ref,
    att_ref, out_ref,
    kv, qv, vv, qt, us, ms, ls, ww, attx, sib, part, relay, fin, outv, tile_of, round_of,
    ra, rb, saz, sax, sbx, sbz, insem, wsem, att_s, att_r, rs_s, relay_r, fin_r, att_o, out_o,
):
    seq = lax.axis_index("seq")
    head = lax.axis_index("head")
    z, x = seq // X, lax.rem(seq, X)
    y, core = head // 2, lax.rem(head, 2)

    def at(zz, xx):
        return lax.rem(zz + 2 * Z, Z) * X + lax.rem(xx + 2 * X, X)

    up, down = at(z + 1, x), at(z - 1, x)
    right, left = at(z, x + 1), at(z, x - 1)
    front = lax.rem(y + 1, Y) * 2 + core
    back = lax.rem(y + 3, Y) * 2 + core
    twin = y * 2 + 1 - core

    load_v = pltpu.make_async_copy(v_ref, vv, insem.at[0])
    load_k = [
        pltpu.make_async_copy(k_ref.at[r], kv.at[r, seq, 0], insem.at[1 + r]) for r in range(ROUNDS)
    ]
    load_q = pltpu.make_async_copy(q_ref, qv, insem.at[3])
    load_w = pltpu.make_async_copy(w_ref, ww.at[0], wsem.at[2])
    load_v.start()
    for load in load_k:
        load.start()
    load_q.start()
    barrier = pltpu.get_barrier_semaphore()
    for peer in (up, down, right, left):
        pl.semaphore_signal(barrier, inc=1, device_id={"seq": peer}, device_id_type=MESH)
    for peer in (front, back, twin):
        pl.semaphore_signal(barrier, inc=1, device_id={"head": peer}, device_id_type=MESH)

    load_v.wait()
    for r in range(ROUNDS):
        for c in range(4):
            rows = slice(c * HEAD, (c + 1) * HEAD)
            kv[r, seq, 1, rows, :] = vv[r, rows, :].T
    for load in load_k:
        load.wait()
    pl.semaphore_wait(barrier, 7)

    def copy_a(r, block, peer, send):
        view = kv.at[r, block, :, pl.ds(0, CUT), :]
        return pltpu.make_async_remote_copy(
            src_ref=view, dst_ref=view, send_sem=send, recv_sem=ra.at[r, block],
            device_id={"seq": peer}, device_id_type=MESH,
        )

    def copy_b(r, block, peer, send):
        view = kv.at[r, block, :, pl.ds(CUT, BLOCK - CUT), :]
        return pltpu.make_async_remote_copy(
            src_ref=view, dst_ref=view, send_sem=send, recv_sem=rb.at[r, block],
            device_id={"seq": peer}, device_id_type=MESH,
        )

    def wait_a(r, block):
        copy_a(r, block, up, saz.at[r, 8]).wait_recv()

    def wait_b(r, block):
        copy_b(r, block, up, sbz.at[r, 32]).wait_recv()

    def launch_b(r, act):
        act(copy_b(r, seq, right, sbx.at[r, 0]))
        act(copy_b(r, seq, left, sbx.at[r, 1]))
        act(copy_b(r, seq, up, sbz.at[r, seq]))
        act(copy_b(r, seq, down, sbz.at[r, 32 + x]))

    def launch_a(r, act):
        act(copy_a(r, seq, up, saz.at[r, z]))
        act(copy_a(r, seq, down, saz.at[r, 8]))
        act(copy_a(r, seq, right, sax.at[r, z, 0]))
        act(copy_a(r, seq, left, sax.at[r, z, 1]))

    def inner_of(k):
        return jnp.logical_and(k > 0, k < Z // 2)

    def below(r, k):
        return jnp.logical_or(
            jnp.logical_and(k == 0, r == 0), jnp.logical_and(k == Z // 2, r == 1)
        )

    def forward_a(r, k, act, waits):
        lo_z, hi_z = lax.rem(z + Z - k, Z), lax.rem(z + k, Z)
        lo, hi = at(lo_z, x), at(hi_z, x)
        if waits:
            wait_a(r, lo)

        @pl.when(jnp.logical_or(k < 3, jnp.logical_and(k == 3, r == 0)))
        def _():
            act(copy_a(r, lo, up, saz.at[r, lo_z]))

        act(copy_a(r, lo, right, sax.at[r, lo_z, 0]))
        act(copy_a(r, lo, left, sax.at[r, lo_z, 1]))

        @pl.when(k < 4)
        def _():
            if waits:
                wait_a(r, hi)

            @pl.when(jnp.logical_or(k < 3, r == 1))
            def _():
                act(copy_a(r, hi, down, saz.at[r, hi_z]))

            act(copy_a(r, hi, right, sax.at[r, hi_z, 0]))
            act(copy_a(r, hi, left, sax.at[r, hi_z, 1]))

    def forward_f(r, k, act, waits):
        lo_z, hi_z = lax.rem(z + Z - k, Z), lax.rem(z + k, Z)
        inner, is_below = inner_of(k), below(r, k)

        @pl.when(jnp.logical_or(inner, is_below))
        def _():
            block = at(lo_z, x - 1)
            if waits:
                wait_a(r, block)
            act(copy_a(r, block, right, sax.at[r, lo_z, 2]))

        @pl.when(jnp.logical_or(inner, jnp.logical_not(is_below)))
        def _():
            block = at(hi_z, x + 1)
            if waits:
                wait_a(r, block)
            act(copy_a(r, block, left, sax.at[r, hi_z, 2]))

    def forward_b(r, k, off, act, waits):
        lo_z, hi_z = lax.rem(z + Z - k, Z), lax.rem(z + k, Z)
        col = lax.rem(x + off, X)
        lo, hi = at(lo_z, col), at(hi_z, col)
        if waits:
            wait_b(r, lo)

        @pl.when(k == 0)
        def _():
            @pl.when(jnp.logical_and(off == 1, r == 1))
            def _():
                act(copy_b(r, lo, left, sbx.at[r, 2]))

            @pl.when(jnp.logical_and(off == 3, r == 0))
            def _():
                act(copy_b(r, lo, right, sbx.at[r, 2]))

            act(copy_b(r, lo, up, sbz.at[r, lo]))
            act(copy_b(r, lo, down, sbz.at[r, 32 + col]))

        @pl.when(k > 0)
        def _():
            @pl.when(jnp.logical_or(k < 3, jnp.logical_and(k == 3, lax.rem(col, 2) == 0)))
            def _():
                act(copy_b(r, lo, up, sbz.at[r, lo]))

            @pl.when(k < 4)
            def _():
                if waits:
                    wait_b(r, hi)

                @pl.when(jnp.logical_or(k < 3, lax.rem(col, 2) == 1))
                def _():
                    act(copy_b(r, hi, down, sbz.at[r, hi]))

    def far_tiles(r, blocks):
        def scores_of(block, cols):
            newer = round_of[block] == 1
            key_tile = jnp.where(newer, kv[r, block, 0], kv[0, block, 0])
            query_t = qt[tile_of[block], :, cols]
            return jnp.dot(key_tile, query_t, preferred_element_type=jnp.float32)

        def mix(block, cols, scores):
            newer = round_of[block] == 1
            value_t = value_rows(jnp.where(newer, kv[r, block, 1], kv[0, block, 1]))
            highest = jnp.max(scores, axis=0, keepdims=True)
            weights = jnp.exp2((scores - highest) * GAIN)
            ms[block, :, cols] = highest
            ls[block, :, cols] = jnp.sum(weights, axis=0, keepdims=True)
            us[block, :, cols] = jnp.dot(
                value_t, weights.astype(jnp.bfloat16), preferred_element_type=jnp.float32
            )

        parts = [(block, slice(c * 256, (c + 1) * 256)) for block in blocks for c in range(2)]
        scores = scores_of(*parts[0])
        for i, part_now in enumerate(parts):
            ahead = scores_of(*parts[i + 1]) if i + 1 < len(parts) else None
            mix(*part_now, scores)
            scores = ahead

    def own_tile(r, h):
        tile = r * HEADS + h
        key_tile = kv[r, seq, 0]
        value_t = value_rows(kv[r, seq, 1])
        parts = []
        for c in range(2):
            cols = slice(c * 256, (c + 1) * 256)
            keys_to = (c + 1) * 256
            scores = jnp.dot(
                key_tile[:keys_to], qt[tile, :, cols], preferred_element_type=jnp.float32
            )
            parts.append((cols, keys_to, scores))
        for cols, keys_to, scores in parts:
            key_at = lax.broadcasted_iota(jnp.int32, scores.shape, 0)
            query_at = lax.broadcasted_iota(jnp.int32, scores.shape, 1) + (keys_to - 256)
            scores = jnp.where(key_at <= query_at, scores, -1e30)
            highest = jnp.max(scores, axis=0, keepdims=True)
            weights = jnp.exp2((scores - highest) * GAIN)
            ms[PEERS + tile, :, cols] = highest
            ls[PEERS + tile, :, cols] = jnp.sum(weights, axis=0, keepdims=True)
            us[PEERS + tile, :, cols] = jnp.dot(
                value_t[:, :keys_to],
                weights.astype(jnp.bfloat16),
                preferred_element_type=jnp.float32,
            )

    def far_slots(r, k, off):
        inner, is_below = inner_of(k), below(r, k)

        def block_of(side):
            return at(jnp.where(side == 0, z + Z - k, z + k), x + off)

        def useful(side):
            live = jnp.logical_or(side == 0, inner)
            return jnp.logical_and(live, jnp.logical_or(r == 0, block_of(side) < seq))

        def arrive(side, carry):
            from_left = jnp.where(inner, side == 0, is_below)
            live = jnp.logical_or(side == 0, inner)
            pending = jnp.logical_or(
                off == 2,
                jnp.logical_or(
                    jnp.logical_and(from_left, off == 1),
                    jnp.logical_and(jnp.logical_not(from_left), off == 3),
                ),
            )

            @pl.when(jnp.logical_and(live, pending))
            def _():
                wait_a(r, block_of(side))

            return carry

        lax.fori_loop(0, 2, arrive, 0)
        both = jnp.logical_and(useful(0), useful(1))

        @pl.when(both)
        def _():
            far_tiles(r, (block_of(0), block_of(1)))

        @pl.when(jnp.logical_not(both))
        def _():
            def one(side, carry):
                @pl.when(useful(side))
                def _():
                    far_tiles(r, (block_of(side),))

                return carry

            lax.fori_loop(0, 2, one, 0)

    def copy_att(r, h):
        return pltpu.make_async_remote_copy(
            src_ref=attx.at[r, 1 - core, h], dst_ref=sib.at[r, h],
            send_sem=att_s.at[r, h], recv_sem=att_r.at[r, h],
            device_id={"head": twin}, device_id_type=MESH,
        )

    def store_att(r, h, c):
        cols = pl.ds(pl.multiple_of(h * HEAD, HEAD), HEAD)
        return pltpu.make_async_copy(
            attx.at[r, c, h], att_ref.at[r, :, c, :, cols], att_o.at[r, h, c]
        )

    def merge(r, h):
        tile = r * HEADS + h
        own = PEERS + tile
        slots, oks = [], []
        top = ms[own]
        for j in range(TOPK):
            chosen = sel_ref[r, j, 0, h]
            ok = chosen < r * PEERS + seq
            slot = jnp.where(ok, lax.rem(chosen, PEERS), 0)
            slots.append(slot)
            oks.append(ok)
            top = jnp.maximum(top, jnp.where(ok, ms[slot], top))
        weights = [jnp.exp2((ms[own] - top) * GAIN)]
        whole = weights[0] * ls[own]
        for slot, ok in zip(slots, oks):
            weight = jnp.where(ok, jnp.exp2(jnp.minimum(ms[slot] - top, 0.0) * GAIN), 0.0)
            weights.append(weight)
            whole = whole + weight * ls[slot]
        row = lax.broadcasted_iota(jnp.int32, (1, BLOCK), 1)
        alive = row < len_ref[0] - (r * PEERS + seq) * BLOCK
        norm = jnp.where(alive, 1.0 / whole, 0.0)
        mixed = us[own] * (weights[0] * norm)
        for slot, weight in zip(slots, weights[1:]):
            mixed = mixed + us[slot] * (weight * norm)
        rows = mixed.T.astype(jnp.bfloat16).reshape(Y, 2, 64, HEAD)
        for c in range(2):
            attx[r, c, h] = rows[:, c]
        copy_att(r, h).start()
        for c in range(2):
            store_att(r, h, c).start()

    def copy_w():
        return pltpu.make_async_remote_copy(
            src_ref=w_ref, dst_ref=ww.at[1], send_sem=wsem.at[0], recv_sem=wsem.at[1],
            device_id={"head": twin}, device_id_type=MESH,
        )

    y_across, y_front, y_back = lax.rem(y + 2, Y), lax.rem(y + 1, Y), lax.rem(y + 3, Y)

    def copy_relay(r, n, side):
        return pltpu.make_async_remote_copy(
            src_ref=part.at[r, n, y_across, side], dst_ref=relay.at[r, n, side],
            send_sem=rs_s.at[r, n, side], recv_sem=relay_r.at[r, n, side],
            device_id={"head": front if side == 0 else back}, device_id_type=MESH,
        )

    def copy_fin(r, n, side, half):
        return pltpu.make_async_remote_copy(
            src_ref=part.at[r, n, y_front if side == 0 else y_back, half],
            dst_ref=fin.at[r, n, side, half],
            send_sem=rs_s.at[r, n, 2 + side * 2 + half], recv_sem=fin_r.at[r, n, side, half],
            device_id={"head": front if side == 0 else back}, device_id_type=MESH,
        )

    def project(r, n):
        rows = [attx[r, core, h].reshape(Y * 64, HEAD) for h in range(HEADS)]
        rows += [sib[r, h].reshape(Y * 64, HEAD) for h in range(HEADS)]
        rows = jnp.concatenate(rows, axis=1)
        for half in range(2):
            cols = pl.ds(pl.multiple_of(n * COLS + half * HALF, HALF), HALF)
            weight = ww[:, :, cols].reshape(2 * HEADS * HEAD, HALF)
            term = jnp.dot(rows, weight, preferred_element_type=jnp.float32)
            part[r, n, :, half] = term.astype(jnp.bfloat16).reshape(Y, 64, HALF)
        copy_relay(r, n, 0).start()
        copy_relay(r, n, 1).start()
        copy_fin(r, n, 0, 1).start()
        copy_fin(r, n, 1, 0).start()

    def pass_on(r, n):
        for side, target, half in ((0, y_front, 0), (1, y_back, 1)):
            copy_relay(r, n, side).wait_recv()
            total = part[r, n, target, half].astype(jnp.float32)
            total = total + relay[r, n, side].astype(jnp.float32)
            part[r, n, target, half] = total.astype(jnp.bfloat16)
            copy_fin(r, n, side, half).start()

    def store_out(r, n):
        cols = pl.ds(pl.multiple_of(n * COLS, COLS), COLS)
        return pltpu.make_async_copy(outv.at[r, :, cols], out_ref.at[r, :, cols], out_o.at[r, n])

    def finish(r, n):
        for side in range(2):
            for half in range(2):
                copy_fin(r, n, side, half).wait_recv()
        for half in range(2):
            total = part[r, n, y, half].astype(jnp.float32)
            total = total + fin[r, n, 0, half].astype(jnp.float32)
            total = total + fin[r, n, 1, half].astype(jnp.float32)
            cols = pl.ds(pl.multiple_of(n * COLS + half * HALF, HALF), HALF)
            outv[r, :, cols] = total.astype(jnp.bfloat16)
        store_out(r, n).start()

    start = lambda copy: copy.start()
    drain = lambda copy: copy.wait_send()

    launch_b(0, start)
    launch_a(0, start)
    copy_w().start()
    load_w.start()

    def table(block, carry):
        tile, newer = jnp.int32(0), jnp.int32(0)
        for r in range(ROUNDS):
            for h in range(HEADS):
                for j in range(TOPK):
                    chosen = sel_ref[r, j, 0, h]
                    hit = jnp.logical_and(
                        lax.rem(chosen, PEERS) == block, chosen < r * PEERS + seq
                    )
                    tile = jnp.where(hit, r * HEADS + h, tile)
                    newer = jnp.where(hit, chosen // PEERS, newer)
        tile_of[block] = tile
        round_of[block] = newer
        return carry

    load_q.wait()
    for r in range(ROUNDS):
        for h in range(HEADS):
            qt[r * HEADS + h] = qv[r, :, h * HEAD : (h + 1) * HEAD].T
    lax.fori_loop(0, PEERS, table, 0)

    def step(t, carry):
        forward, work_code = jnp.int32(FORWARD[0]), jnp.int32(WORK[0])
        third = t // 3
        for w in range(1, len(FORWARD)):
            here = third == w
            forward = jnp.where(here, FORWARD[w], forward)
            work_code = jnp.where(here, WORK[w], work_code)
        bits = lax.rem(t, 3) * 9
        forward, work_code = forward >> bits, work_code >> bits
        kind, r, k, off = forward & 7, (forward >> 3) & 1, (forward >> 4) & 7, (forward >> 7) & 3

        @pl.when(kind == 1)
        def _():
            forward_a(r, k, start, True)

        @pl.when(kind == 2)
        def _():
            forward_f(r, k, start, True)

        @pl.when(kind == 3)
        def _():
            forward_b(r, k, off, start, True)

        @pl.when(kind == 4)
        def _():
            launch_a(1, start)

        @pl.when(kind == 5)
        def _():
            launch_b(1, start)

        work, wr = work_code & 7, (work_code >> 3) & 1
        item, woff = (work_code >> 4) & 7, (work_code >> 7) & 3

        @pl.when(work == 1)
        def _():
            far_slots(wr, item, woff)

        @pl.when(work == 2)
        def _():
            own_tile(wr, item)

        @pl.when(work == 3)
        def _():
            merge(wr, item)

        @pl.when(work == 4)
        def _():
            @pl.when(item == 0)
            def _():
                @pl.when(wr == 0)
                def _():
                    load_w.wait()
                    copy_w().wait_recv()

                for h in range(HEADS):
                    copy_att(wr, h).wait_recv()

            project(wr, item)

        @pl.when(work == 5)
        def _():
            pass_on(wr, item)

        @pl.when(work == 6)
        def _():
            finish(wr, item)

        return carry

    lax.fori_loop(0, STEPS, step, 0)

    def drain_step(t, carry):
        r, k, off = t // 20, lax.rem(t // 4, 5), lax.rem(t, 4)

        @pl.when(jnp.logical_or(k > 0, off > 0))
        def _():
            forward_b(r, k, off, drain, False)

        @pl.when(off == 0)
        def _():
            forward_f(r, k, drain, False)

        @pl.when(jnp.logical_and(off == 0, k > 0))
        def _():
            forward_a(r, k, drain, False)

        return carry

    for r in range(ROUNDS):
        launch_a(r, drain)
        launch_b(r, drain)
    lax.fori_loop(0, ROUNDS * 20, drain_step, 0)
    copy_w().wait_send()

    def drain_sum(t, carry):
        r, n = t // TILES, lax.rem(t, TILES)
        copy_att(r, n).wait_send()
        for c in range(2):
            store_att(r, n, c).wait()
        for side in range(2):
            copy_relay(r, n, side).wait_send()
            for half in range(2):
                copy_fin(r, n, side, half).wait_send()
        store_out(r, n).wait()
        return carry

    lax.fori_loop(0, ROUNDS * TILES, drain_sum, 0)


def hand_over(att_in, out_in, att_ref, out_ref, att_v, out_v, sems):
    places = []
    for r in range(ROUNDS):
        for i in range(2):
            rows = slice(i * 256, (i + 1) * 256)
            places.append((att_in, att_v, att_ref, r, rows))
            rows = slice(i * 32, (i + 1) * 32)
            places.append((out_in, out_v, out_ref, r, rows))
    loads, stores = [], []
    for i, (src, mid, dst, r, rows) in enumerate(places):
        loads.append(
            pltpu.make_async_copy(src.at[r, rows, :], mid.at[r, rows, :], sems.at[0, i])
        )
        stores.append(
            pltpu.make_async_copy(mid.at[r, rows, :], dst.at[r, rows, :], sems.at[1, i])
        )
    for load in loads:
        load.start()
    for load, store in zip(loads, stores):
        load.wait()
        store.start()
    for store in stores:
        store.wait()


def per_device(queries, keys, values, selected, length, out_weight):
    anywhere = pl.BlockSpec(memory_space=pl.ANY)
    smem = pl.BlockSpec(memory_space=pltpu.SMEM)
    bf16, f32 = jnp.bfloat16, jnp.float32
    dma = pltpu.SemaphoreType.DMA
    attended, projected = pl.pallas_call(
        kernel,
        out_shape=(
            jax.ShapeDtypeStruct((ROUNDS, Y, 2, 64, HEADS * HEAD), bf16),
            jax.ShapeDtypeStruct((ROUNDS, 64, MODEL), bf16),
        ),
        in_specs=[smem, smem, anywhere, anywhere, anywhere, anywhere],
        out_specs=(anywhere, anywhere),
        scratch_shapes=[
            pltpu.VMEM((ROUNDS, PEERS, 2, BLOCK, HEAD), bf16),
            pltpu.VMEM((ROUNDS, BLOCK, HEADS * HEAD), bf16),
            pltpu.VMEM((ROUNDS, BLOCK, HEAD), bf16),
            pltpu.VMEM((ROUNDS * HEADS, HEAD, BLOCK), bf16),
            pltpu.VMEM((PEERS + ROUNDS * HEADS, HEAD, BLOCK), f32),
            pltpu.VMEM((PEERS + ROUNDS * HEADS, 1, BLOCK), f32),
            pltpu.VMEM((PEERS + ROUNDS * HEADS, 1, BLOCK), f32),
            pltpu.VMEM((2, HEADS * HEAD, MODEL), bf16),
            pltpu.VMEM((ROUNDS, 2, HEADS, Y, 64, HEAD), bf16),
            pltpu.VMEM((ROUNDS, HEADS, Y, 64, HEAD), bf16),
            pltpu.VMEM((ROUNDS, TILES, Y, 2, 64, HALF), bf16),
            pltpu.VMEM((ROUNDS, TILES, 2, 64, HALF), bf16),
            pltpu.VMEM((ROUNDS, TILES, 2, 2, 64, HALF), bf16),
            pltpu.VMEM((ROUNDS, 64, MODEL), bf16),
            pltpu.SMEM((PEERS,), jnp.int32),
            pltpu.SMEM((PEERS,), jnp.int32),
            dma((ROUNDS, PEERS)),
            dma((ROUNDS, PEERS)),
            dma((ROUNDS, Z + 1)),
            dma((ROUNDS, Z, 3)),
            dma((ROUNDS, 3)),
            dma((ROUNDS, PEERS + X)),
            dma((4,)),
            dma((3,)),
            dma((ROUNDS, HEADS)),
            dma((ROUNDS, HEADS)),
            dma((ROUNDS, TILES, 6)),
            dma((ROUNDS, TILES, 2)),
            dma((ROUNDS, TILES, 2, 2)),
            dma((ROUNDS, HEADS, 2)),
            dma((ROUNDS, TILES)),
        ],
        compiler_params=pltpu.CompilerParams(
            collective_id=0, has_side_effects=True, vmem_limit_bytes=60 * 1024 * 1024
        ),
        cost_estimate=pl.CostEstimate(
            flops=72 * 4 * BLOCK * BLOCK * HEAD,
            bytes_accessed=8 * 1024 * 1024,
            transcendentals=72 * BLOCK * BLOCK,
        ),
        name="attend_and_project",
    )(selected.transpose(0, 3, 1, 2), length, queries, keys, values, out_weight)
    attended = attended.reshape(ROUNDS, BLOCK, HEADS * HEAD)
    return pl.pallas_call(
        hand_over,
        out_shape=(
            jax.ShapeDtypeStruct(attended.shape, bf16),
            jax.ShapeDtypeStruct(projected.shape, bf16),
        ),
        in_specs=[anywhere, anywhere],
        out_specs=(anywhere, anywhere),
        scratch_shapes=[
            pltpu.VMEM(attended.shape, bf16),
            pltpu.VMEM(projected.shape, bf16),
            dma((2, 8)),
        ],
        compiler_params=pltpu.CompilerParams(vmem_limit_bytes=60 * 1024 * 1024),
        name="hand_over",
    )(attended, projected)


def solution(mesh):
    placed = (
        P(None, "seq", "head"),
        P(None, "seq", "head"),
        P(None, "seq", "head"),
        P(None, "seq", "head", None),
        P(),
        P("head", None),
    )
    return jax.shard_map(
        per_device,
        mesh=mesh,
        in_specs=placed,
        out_specs=(P(None, "seq", "head"), P(None, ("seq", "head"), None)),
        check_vma=False,
    )
```

```python
import jax
import jax.numpy as jnp
from jax import lax
from jax.experimental import pallas as pl
from jax.experimental.pallas import tpu as pltpu
from jax.sharding import PartitionSpec as P

HEAD = 128
Z, X, Y = 8, 4, 4
PEERS = Z * X
BLOCK = 512
HEADS = 4
TOPK = 3
ROUNDS = 2
MODEL = 4096
GAIN = HEAD ** (-0.5) * 1.4426950408889634
CUT = 304
COLS = 1024
HALF = COLS // 2
TILES = MODEL // COLS
MESH = pl.DeviceIdType.MESH
STEPS = 100
FORWARD = (
    4457859, 5113475, 4793889, 206336, 72107008, 9200291, 3360547, 6721,
    114058240, 80504499, 36450816, 103777819, 51118146, 17729034, 10747904, 13579,
    155, 15152640, 74186795, 19224491, 42, 78411264, 29696, 19398656,
    49021371, 38400, 53450555, 169472, 0, 0, 0, 0,
    0, 0,
)
WORK = (
    8912896, 0, 524314, 67379754, 15278593, 0, 100925449, 71771041,
    33833482, 4718592, 82609, 103022881, 25905, 35913728, 221761, 117727744,
    9274177, 1050377, 18452, 26624, 9720489, 5505177, 6583209, 209446,
    14037945, 19139257, 52925225, 11440953, 7346187, 15751222, 7608838, 11803709,
    16264222, 46,
)


def value_rows(stacked):
    return jnp.concatenate([stacked[c * HEAD : (c + 1) * HEAD] for c in range(4)], axis=1)


def kernel(
    sel_ref, len_ref, q_ref, k_ref, v_ref, w_ref,
    att_ref, out_ref,
    kv, qv, vv, qt, us, ms, ls, ww, attx, sib, part, relay, fin, outv, tile_of, round_of,
    ra, rb, saz, sax, sbx, sbz, insem, wsem, att_s, att_r, rs_s, relay_r, fin_r, att_o, out_o,
):
    seq = lax.axis_index("seq")
    head = lax.axis_index("head")
    z, x = seq // X, lax.rem(seq, X)
    y, core = head // 2, lax.rem(head, 2)

    def at(zz, xx):
        return lax.rem(zz + 2 * Z, Z) * X + lax.rem(xx + 2 * X, X)

    up, down = at(z + 1, x), at(z - 1, x)
    right, left = at(z, x + 1), at(z, x - 1)
    front = lax.rem(y + 1, Y) * 2 + core
    back = lax.rem(y + 3, Y) * 2 + core
    twin = y * 2 + 1 - core

    load_v = pltpu.make_async_copy(v_ref, vv, insem.at[0])
    load_k = [
        pltpu.make_async_copy(k_ref.at[r], kv.at[r, seq, 0], insem.at[1 + r]) for r in range(ROUNDS)
    ]
    load_q = pltpu.make_async_copy(q_ref, qv, insem.at[3])
    load_w = pltpu.make_async_copy(w_ref, ww.at[0], wsem.at[2])
    load_v.start()
    for load in load_k:
        load.start()
    load_q.start()
    barrier = pltpu.get_barrier_semaphore()
    for peer in (up, down, right, left):
        pl.semaphore_signal(barrier, inc=1, device_id={"seq": peer}, device_id_type=MESH)
    for peer in (front, back, twin):
        pl.semaphore_signal(barrier, inc=1, device_id={"head": peer}, device_id_type=MESH)

    load_v.wait()
    for r in range(ROUNDS):
        for c in range(4):
            rows = slice(c * HEAD, (c + 1) * HEAD)
            kv[r, seq, 1, rows, :] = vv[r, rows, :].T
    for load in load_k:
        load.wait()
    pl.semaphore_wait(barrier, 7)

    def copy_a(r, block, peer, send):
        view = kv.at[r, block, :, pl.ds(0, CUT), :]
        return pltpu.make_async_remote_copy(
            src_ref=view, dst_ref=view, send_sem=send, recv_sem=ra.at[r, block],
            device_id={"seq": peer}, device_id_type=MESH,
        )

    def copy_b(r, block, peer, send):
        view = kv.at[r, block, :, pl.ds(CUT, BLOCK - CUT), :]
        return pltpu.make_async_remote_copy(
            src_ref=view, dst_ref=view, send_sem=send, recv_sem=rb.at[r, block],
            device_id={"seq": peer}, device_id_type=MESH,
        )

    def wait_a(r, block):
        copy_a(r, block, up, saz.at[r, 8]).wait_recv()

    def wait_b(r, block):
        copy_b(r, block, up, sbz.at[r, 32]).wait_recv()

    def launch_b(r, act):
        act(copy_b(r, seq, right, sbx.at[r, 0]))
        act(copy_b(r, seq, left, sbx.at[r, 1]))
        act(copy_b(r, seq, up, sbz.at[r, seq]))
        act(copy_b(r, seq, down, sbz.at[r, 32 + x]))

    def launch_a(r, act):
        act(copy_a(r, seq, up, saz.at[r, z]))
        act(copy_a(r, seq, down, saz.at[r, 8]))
        act(copy_a(r, seq, right, sax.at[r, z, 0]))
        act(copy_a(r, seq, left, sax.at[r, z, 1]))

    def inner_of(k):
        return jnp.logical_and(k > 0, k < Z // 2)

    def below(r, k):
        return jnp.logical_or(
            jnp.logical_and(k == 0, r == 0), jnp.logical_and(k == Z // 2, r == 1)
        )

    def forward_a(r, k, act, waits):
        lo_z, hi_z = lax.rem(z + Z - k, Z), lax.rem(z + k, Z)
        lo, hi = at(lo_z, x), at(hi_z, x)
        if waits:
            wait_a(r, lo)

        @pl.when(jnp.logical_or(k < 3, jnp.logical_and(k == 3, r == 0)))
        def _():
            act(copy_a(r, lo, up, saz.at[r, lo_z]))

        act(copy_a(r, lo, right, sax.at[r, lo_z, 0]))
        act(copy_a(r, lo, left, sax.at[r, lo_z, 1]))

        @pl.when(k < 4)
        def _():
            if waits:
                wait_a(r, hi)

            @pl.when(jnp.logical_or(k < 3, r == 1))
            def _():
                act(copy_a(r, hi, down, saz.at[r, hi_z]))

            act(copy_a(r, hi, right, sax.at[r, hi_z, 0]))
            act(copy_a(r, hi, left, sax.at[r, hi_z, 1]))

    def forward_f(r, k, act, waits):
        lo_z, hi_z = lax.rem(z + Z - k, Z), lax.rem(z + k, Z)
        inner, is_below = inner_of(k), below(r, k)

        @pl.when(jnp.logical_or(inner, is_below))
        def _():
            block = at(lo_z, x - 1)
            if waits:
                wait_a(r, block)
            act(copy_a(r, block, right, sax.at[r, lo_z, 2]))

        @pl.when(jnp.logical_or(inner, jnp.logical_not(is_below)))
        def _():
            block = at(hi_z, x + 1)
            if waits:
                wait_a(r, block)
            act(copy_a(r, block, left, sax.at[r, hi_z, 2]))

    def forward_b(r, k, off, act, waits):
        lo_z, hi_z = lax.rem(z + Z - k, Z), lax.rem(z + k, Z)
        col = lax.rem(x + off, X)
        lo, hi = at(lo_z, col), at(hi_z, col)
        if waits:
            wait_b(r, lo)

        @pl.when(k == 0)
        def _():
            @pl.when(jnp.logical_and(off == 1, r == 1))
            def _():
                act(copy_b(r, lo, left, sbx.at[r, 2]))

            @pl.when(jnp.logical_and(off == 3, r == 0))
            def _():
                act(copy_b(r, lo, right, sbx.at[r, 2]))

            act(copy_b(r, lo, up, sbz.at[r, lo]))
            act(copy_b(r, lo, down, sbz.at[r, 32 + col]))

        @pl.when(k > 0)
        def _():
            @pl.when(jnp.logical_or(k < 3, jnp.logical_and(k == 3, lax.rem(col, 2) == 0)))
            def _():
                act(copy_b(r, lo, up, sbz.at[r, lo]))

            @pl.when(k < 4)
            def _():
                if waits:
                    wait_b(r, hi)

                @pl.when(jnp.logical_or(k < 3, lax.rem(col, 2) == 1))
                def _():
                    act(copy_b(r, hi, down, sbz.at[r, hi]))

    def far_tiles(r, blocks):
        def scores_of(block, cols):
            newer = round_of[block] == 1
            key_tile = jnp.where(newer, kv[r, block, 0], kv[0, block, 0])
            query_t = qt[tile_of[block], :, cols]
            return jnp.dot(key_tile, query_t, preferred_element_type=jnp.float32)

        def mix(block, cols, scores):
            newer = round_of[block] == 1
            value_t = value_rows(jnp.where(newer, kv[r, block, 1], kv[0, block, 1]))
            highest = jnp.max(scores, axis=0, keepdims=True)
            weights = jnp.exp2((scores - highest) * GAIN)
            ms[block, :, cols] = highest
            ls[block, :, cols] = jnp.sum(weights, axis=0, keepdims=True)
            us[block, :, cols] = jnp.dot(
                value_t, weights.astype(jnp.bfloat16), preferred_element_type=jnp.float32
            )

        parts = [(block, slice(c * 256, (c + 1) * 256)) for block in blocks for c in range(2)]
        scores = scores_of(*parts[0])
        for i, part_now in enumerate(parts):
            ahead = scores_of(*parts[i + 1]) if i + 1 < len(parts) else None
            mix(*part_now, scores)
            scores = ahead

    def own_tile(r, h):
        tile = r * HEADS + h
        key_tile = kv[r, seq, 0]
        value_t = value_rows(kv[r, seq, 1])
        parts = []
        for c in range(2):
            cols = slice(c * 256, (c + 1) * 256)
            keys_to = (c + 1) * 256
            scores = jnp.dot(
                key_tile[:keys_to], qt[tile, :, cols], preferred_element_type=jnp.float32
            )
            parts.append((cols, keys_to, scores))
        for cols, keys_to, scores in parts:
            key_at = lax.broadcasted_iota(jnp.int32, scores.shape, 0)
            query_at = lax.broadcasted_iota(jnp.int32, scores.shape, 1) + (keys_to - 256)
            scores = jnp.where(key_at <= query_at, scores, -1e30)
            highest = jnp.max(scores, axis=0, keepdims=True)
            weights = jnp.exp2((scores - highest) * GAIN)
            ms[PEERS + tile, :, cols] = highest
            ls[PEERS + tile, :, cols] = jnp.sum(weights, axis=0, keepdims=True)
            us[PEERS + tile, :, cols] = jnp.dot(
                value_t[:, :keys_to],
                weights.astype(jnp.bfloat16),
                preferred_element_type=jnp.float32,
            )

    def far_slots(r, k, off):
        inner, is_below = inner_of(k), below(r, k)

        def block_of(side):
            return at(jnp.where(side == 0, z + Z - k, z + k), x + off)

        def useful(side):
            live = jnp.logical_or(side == 0, inner)
            return jnp.logical_and(live, jnp.logical_or(r == 0, block_of(side) < seq))

        def arrive(side, carry):
            from_left = jnp.where(inner, side == 0, is_below)
            live = jnp.logical_or(side == 0, inner)
            pending = jnp.logical_or(
                off == 2,
                jnp.logical_or(
                    jnp.logical_and(from_left, off == 1),
                    jnp.logical_and(jnp.logical_not(from_left), off == 3),
                ),
            )

            @pl.when(jnp.logical_and(live, pending))
            def _():
                wait_a(r, block_of(side))

            return carry

        lax.fori_loop(0, 2, arrive, 0)
        both = jnp.logical_and(useful(0), useful(1))

        @pl.when(both)
        def _():
            far_tiles(r, (block_of(0), block_of(1)))

        @pl.when(jnp.logical_not(both))
        def _():
            def one(side, carry):
                @pl.when(useful(side))
                def _():
                    far_tiles(r, (block_of(side),))

                return carry

            lax.fori_loop(0, 2, one, 0)

    def copy_att(r, h):
        return pltpu.make_async_remote_copy(
            src_ref=attx.at[r, 1 - core, h], dst_ref=sib.at[r, h],
            send_sem=att_s.at[r, h], recv_sem=att_r.at[r, h],
            device_id={"head": twin}, device_id_type=MESH,
        )

    def store_att(r, h, c):
        cols = pl.ds(pl.multiple_of(h * HEAD, HEAD), HEAD)
        return pltpu.make_async_copy(
            attx.at[r, c, h], att_ref.at[r, :, c, :, cols], att_o.at[r, h, c]
        )

    def merge(r, h):
        tile = r * HEADS + h
        own = PEERS + tile
        slots, oks = [], []
        top = ms[own]
        for j in range(TOPK):
            chosen = sel_ref[r, j, 0, h]
            ok = chosen < r * PEERS + seq
            slot = jnp.where(ok, lax.rem(chosen, PEERS), 0)
            slots.append(slot)
            oks.append(ok)
            top = jnp.maximum(top, jnp.where(ok, ms[slot], top))
        weights = [jnp.exp2((ms[own] - top) * GAIN)]
        whole = weights[0] * ls[own]
        for slot, ok in zip(slots, oks):
            weight = jnp.where(ok, jnp.exp2(jnp.minimum(ms[slot] - top, 0.0) * GAIN), 0.0)
            weights.append(weight)
            whole = whole + weight * ls[slot]
        row = lax.broadcasted_iota(jnp.int32, (1, BLOCK), 1)
        alive = row < len_ref[0] - (r * PEERS + seq) * BLOCK
        norm = jnp.where(alive, 1.0 / whole, 0.0)
        mixed = us[own] * (weights[0] * norm)
        for slot, weight in zip(slots, weights[1:]):
            mixed = mixed + us[slot] * (weight * norm)
        rows = mixed.astype(jnp.bfloat16).T.reshape(Y, 2, 64, HEAD)
        for c in range(2):
            attx[r, c, h] = rows[:, c]
        copy_att(r, h).start()
        for c in range(2):
            store_att(r, h, c).start()

    def copy_w():
        return pltpu.make_async_remote_copy(
            src_ref=w_ref, dst_ref=ww.at[1], send_sem=wsem.at[0], recv_sem=wsem.at[1],
            device_id={"head": twin}, device_id_type=MESH,
        )

    y_across, y_front, y_back = lax.rem(y + 2, Y), lax.rem(y + 1, Y), lax.rem(y + 3, Y)

    def copy_relay(r, n, side):
        return pltpu.make_async_remote_copy(
            src_ref=part.at[r, n, y_across, side], dst_ref=relay.at[r, n, side],
            send_sem=rs_s.at[r, n, side], recv_sem=relay_r.at[r, n, side],
            device_id={"head": front if side == 0 else back}, device_id_type=MESH,
        )

    def copy_fin(r, n, side, half):
        return pltpu.make_async_remote_copy(
            src_ref=part.at[r, n, y_front if side == 0 else y_back, half],
            dst_ref=fin.at[r, n, side, half],
            send_sem=rs_s.at[r, n, 2 + side * 2 + half], recv_sem=fin_r.at[r, n, side, half],
            device_id={"head": front if side == 0 else back}, device_id_type=MESH,
        )

    def project(r, n):
        rows = [attx[r, core, h].reshape(Y * 64, HEAD) for h in range(HEADS)]
        rows += [sib[r, h].reshape(Y * 64, HEAD) for h in range(HEADS)]
        rows = jnp.concatenate(rows, axis=1)
        for half in range(2):
            cols = pl.ds(pl.multiple_of(n * COLS + half * HALF, HALF), HALF)
            weight = ww[:, :, cols].reshape(2 * HEADS * HEAD, HALF)
            term = jnp.dot(rows, weight, preferred_element_type=jnp.float32)
            part[r, n, :, half] = term.astype(jnp.bfloat16).reshape(Y, 64, HALF)
        copy_relay(r, n, 0).start()
        copy_relay(r, n, 1).start()
        copy_fin(r, n, 0, 1).start()
        copy_fin(r, n, 1, 0).start()

    def pass_on(r, n):
        for side, target, half in ((0, y_front, 0), (1, y_back, 1)):
            copy_relay(r, n, side).wait_recv()
            total = part[r, n, target, half].astype(jnp.float32)
            total = total + relay[r, n, side].astype(jnp.float32)
            part[r, n, target, half] = total.astype(jnp.bfloat16)
            copy_fin(r, n, side, half).start()

    def store_out(r, n):
        cols = pl.ds(pl.multiple_of(n * COLS, COLS), COLS)
        return pltpu.make_async_copy(outv.at[r, :, cols], out_ref.at[r, :, cols], out_o.at[r, n])

    def finish(r, n):
        for side in range(2):
            for half in range(2):
                copy_fin(r, n, side, half).wait_recv()
        for half in range(2):
            total = part[r, n, y, half].astype(jnp.float32)
            total = total + fin[r, n, 0, half].astype(jnp.float32)
            total = total + fin[r, n, 1, half].astype(jnp.float32)
            cols = pl.ds(pl.multiple_of(n * COLS + half * HALF, HALF), HALF)
            outv[r, :, cols] = total.astype(jnp.bfloat16)
        store_out(r, n).start()

    start = lambda copy: copy.start()
    drain = lambda copy: copy.wait_send()

    launch_b(0, start)
    launch_a(0, start)
    copy_w().start()
    load_w.start()

    def table(block, carry):
        tile, newer = jnp.int32(0), jnp.int32(0)
        for r in range(ROUNDS):
            for h in range(HEADS):
                for j in range(TOPK):
                    chosen = sel_ref[r, j, 0, h]
                    hit = jnp.logical_and(
                        lax.rem(chosen, PEERS) == block, chosen < r * PEERS + seq
                    )
                    tile = jnp.where(hit, r * HEADS + h, tile)
                    newer = jnp.where(hit, chosen // PEERS, newer)
        tile_of[block] = tile
        round_of[block] = newer
        return carry

    load_q.wait()
    for r in range(ROUNDS):
        for h in range(HEADS):
            qt[r * HEADS + h] = qv[r, :, h * HEAD : (h + 1) * HEAD].T
    lax.fori_loop(0, PEERS, table, 0)

    def step(t, carry):
        forward, work_code = jnp.int32(FORWARD[0]), jnp.int32(WORK[0])
        third = t // 3
        for w in range(1, len(FORWARD)):
            here = third == w
            forward = jnp.where(here, FORWARD[w], forward)
            work_code = jnp.where(here, WORK[w], work_code)
        bits = lax.rem(t, 3) * 9
        forward, work_code = forward >> bits, work_code >> bits
        kind, r, k, off = forward & 7, (forward >> 3) & 1, (forward >> 4) & 7, (forward >> 7) & 3

        @pl.when(kind == 1)
        def _():
            forward_a(r, k, start, True)

        @pl.when(kind == 2)
        def _():
            forward_f(r, k, start, True)

        @pl.when(kind == 3)
        def _():
            forward_b(r, k, off, start, True)

        @pl.when(kind == 4)
        def _():
            launch_a(1, start)

        @pl.when(kind == 5)
        def _():
            launch_b(1, start)

        work, wr = work_code & 7, (work_code >> 3) & 1
        item, woff = (work_code >> 4) & 7, (work_code >> 7) & 3

        @pl.when(work == 1)
        def _():
            far_slots(wr, item, woff)

        @pl.when(work == 2)
        def _():
            own_tile(wr, item)

        @pl.when(work == 3)
        def _():
            merge(wr, item)
            merge(wr, item + 1)

        @pl.when(work == 4)
        def _():
            @pl.when(item == 0)
            def _():
                @pl.when(wr == 0)
                def _():
                    load_w.wait()
                    copy_w().wait_recv()

                for h in range(HEADS):
                    copy_att(wr, h).wait_recv()

            project(wr, item)

        @pl.when(work == 5)
        def _():
            pass_on(wr, item)

        @pl.when(work == 6)
        def _():
            finish(wr, item)

        return carry

    lax.fori_loop(0, STEPS, step, 0)

    def drain_step(t, carry):
        r, k, off = t // 20, lax.rem(t // 4, 5), lax.rem(t, 4)

        @pl.when(jnp.logical_or(k > 0, off > 0))
        def _():
            forward_b(r, k, off, drain, False)

        @pl.when(off == 0)
        def _():
            forward_f(r, k, drain, False)

        @pl.when(jnp.logical_and(off == 0, k > 0))
        def _():
            forward_a(r, k, drain, False)

        return carry

    for r in range(ROUNDS):
        launch_a(r, drain)
        launch_b(r, drain)
    lax.fori_loop(0, ROUNDS * 20, drain_step, 0)
    copy_w().wait_send()

    def drain_sum(t, carry):
        r, n = t // TILES, lax.rem(t, TILES)
        copy_att(r, n).wait_send()
        for c in range(2):
            store_att(r, n, c).wait()
        for side in range(2):
            copy_relay(r, n, side).wait_send()
            for half in range(2):
                copy_fin(r, n, side, half).wait_send()
        store_out(r, n).wait()
        return carry

    lax.fori_loop(0, ROUNDS * TILES, drain_sum, 0)


def hand_over(att_in, out_in, att_ref, out_ref, att_v, out_v, sems):
    places = []
    for r in range(ROUNDS):
        for i in range(2):
            rows = slice(i * 256, (i + 1) * 256)
            places.append((att_in, att_v, att_ref, r, rows))
            rows = slice(i * 32, (i + 1) * 32)
            places.append((out_in, out_v, out_ref, r, rows))
    loads, stores = [], []
    for i, (src, mid, dst, r, rows) in enumerate(places):
        loads.append(
            pltpu.make_async_copy(src.at[r, rows, :], mid.at[r, rows, :], sems.at[0, i])
        )
        stores.append(
            pltpu.make_async_copy(mid.at[r, rows, :], dst.at[r, rows, :], sems.at[1, i])
        )
    for load in loads:
        load.start()
    for load, store in zip(loads, stores):
        load.wait()
        store.start()
    for store in stores:
        store.wait()


def per_device(queries, keys, values, selected, length, out_weight):
    anywhere = pl.BlockSpec(memory_space=pl.ANY)
    smem = pl.BlockSpec(memory_space=pltpu.SMEM)
    bf16, f32 = jnp.bfloat16, jnp.float32
    dma = pltpu.SemaphoreType.DMA
    attended, projected = pl.pallas_call(
        kernel,
        out_shape=(
            jax.ShapeDtypeStruct((ROUNDS, Y, 2, 64, HEADS * HEAD), bf16),
            jax.ShapeDtypeStruct((ROUNDS, 64, MODEL), bf16),
        ),
        in_specs=[smem, smem, anywhere, anywhere, anywhere, anywhere],
        out_specs=(anywhere, anywhere),
        scratch_shapes=[
            pltpu.VMEM((ROUNDS, PEERS, 2, BLOCK, HEAD), bf16),
            pltpu.VMEM((ROUNDS, BLOCK, HEADS * HEAD), bf16),
            pltpu.VMEM((ROUNDS, BLOCK, HEAD), bf16),
            pltpu.VMEM((ROUNDS * HEADS, HEAD, BLOCK), bf16),
            pltpu.VMEM((PEERS + ROUNDS * HEADS, HEAD, BLOCK), f32),
            pltpu.VMEM((PEERS + ROUNDS * HEADS, 1, BLOCK), f32),
            pltpu.VMEM((PEERS + ROUNDS * HEADS, 1, BLOCK), f32),
            pltpu.VMEM((2, HEADS * HEAD, MODEL), bf16),
            pltpu.VMEM((ROUNDS, 2, HEADS, Y, 64, HEAD), bf16),
            pltpu.VMEM((ROUNDS, HEADS, Y, 64, HEAD), bf16),
            pltpu.VMEM((ROUNDS, TILES, Y, 2, 64, HALF), bf16),
            pltpu.VMEM((ROUNDS, TILES, 2, 64, HALF), bf16),
            pltpu.VMEM((ROUNDS, TILES, 2, 2, 64, HALF), bf16),
            pltpu.VMEM((ROUNDS, 64, MODEL), bf16),
            pltpu.SMEM((PEERS,), jnp.int32),
            pltpu.SMEM((PEERS,), jnp.int32),
            dma((ROUNDS, PEERS)),
            dma((ROUNDS, PEERS)),
            dma((ROUNDS, Z + 1)),
            dma((ROUNDS, Z, 3)),
            dma((ROUNDS, 3)),
            dma((ROUNDS, PEERS + X)),
            dma((4,)),
            dma((3,)),
            dma((ROUNDS, HEADS)),
            dma((ROUNDS, HEADS)),
            dma((ROUNDS, TILES, 6)),
            dma((ROUNDS, TILES, 2)),
            dma((ROUNDS, TILES, 2, 2)),
            dma((ROUNDS, HEADS, 2)),
            dma((ROUNDS, TILES)),
        ],
        compiler_params=pltpu.CompilerParams(
            collective_id=0, has_side_effects=True, vmem_limit_bytes=60 * 1024 * 1024
        ),
        cost_estimate=pl.CostEstimate(
            flops=72 * 4 * BLOCK * BLOCK * HEAD,
            bytes_accessed=8 * 1024 * 1024,
            transcendentals=72 * BLOCK * BLOCK,
        ),
        name="attend_and_project",
    )(selected.transpose(0, 3, 1, 2), length, queries, keys, values, out_weight)
    attended = attended.reshape(ROUNDS, BLOCK, HEADS * HEAD)
    return pl.pallas_call(
        hand_over,
        out_shape=(
            jax.ShapeDtypeStruct(attended.shape, bf16),
            jax.ShapeDtypeStruct(projected.shape, bf16),
        ),
        in_specs=[anywhere, anywhere],
        out_specs=(anywhere, anywhere),
        scratch_shapes=[
            pltpu.VMEM(attended.shape, bf16),
            pltpu.VMEM(projected.shape, bf16),
            dma((2, 8)),
        ],
        compiler_params=pltpu.CompilerParams(vmem_limit_bytes=60 * 1024 * 1024),
        name="hand_over",
    )(attended, projected)


def solution(mesh):
    placed = (
        P(None, "seq", "head"),
        P(None, "seq", "head"),
        P(None, "seq", "head"),
        P(None, "seq", "head", None),
        P(),
        P("head", None),
    )
    return jax.shard_map(
        per_device,
        mesh=mesh,
        in_specs=placed,
        out_specs=(P(None, "seq", "head"), P(None, ("seq", "head"), None)),
        check_vma=False,
    )
```
